256 devices in a mesh: fac: 64 (over y, x_lo, z), chan: 4 (over x_hi, core).
Axes of the slice: x: 4 (x_hi: 2, x_lo: 2; x = x_hi * 2 + x_lo), y: 4, z: 8, core: 2. Of those that a mesh axis runs over, the one named last changes fastest.
Arguments:
- primal_image: float32 [64, 1024, 2048], P('chan', 'fac'), may hold values from 0 to 1
- dual_coef: float32 [4, 64, 512, 1024], P(None, 'chan', 'fac'), may hold values from -6 to 6
- l21_weight: float32 [4, 512, 1024], P(None, 'fac'), may hold values from 2 to 16
- visibilities: bfloat16 [64, 16384], P('fac', 'chan'), may hold values from -6 to 6
- tile_index: int32 [64, 16384], P('fac', 'chan'), may hold values from 0 to 4095
- kernel_values: bfloat16 [64, 16384, 128], P('fac', 'chan'), may hold values from -6 to 6
- kernel_pattern: int32 [64, 16384, 128], P('fac', 'chan'), may hold values 0 or 1
Outputs:
- image_next: float32 [64, 1024, 2048], P('chan', 'fac')
- dual_next: float32 [4, 64, 512, 1024], P(None, 'chan', 'fac')
The draws below stay inside these ranges and needn't reach their ends.
All inputs are finite; a program needn't handle non-finite values. No bound on the sum of `kernel_pattern` on one device may be relied on, other than what follows from the above.
Results may differ from the reference program's by a relative error of at most 0.00035.
Values sent between devices are 32-bit elements; how exact they have to be, the bound alone decides.
No kernel may reach another device: no remote copies, remote signals or barrier semaphores. Data moves between devices by JAX's collectives and lax.ppermute only.
A program may use at most 128 MiB of HBM per device.

```python
import math
import jax
import jax.numpy as jnp
from jax import lax

NCH = 64
NX = 2048
VIS_DEV = 4096
NY = 1024
NVIS = 16384
NTILE = 4096
N_CHAN = 4


def touch_ends(values, key, low, high):
    longest = values.shape.index(max(values.shape))
    spots = []
    for shift in (0, 1):
        where = [jax.random.randint(jax.random.fold_in(key, axis), (), 0, length) for axis, length in enumerate(values.shape)]
        where[longest] = (where[longest] + shift) % values.shape[longest]
        spots.append(tuple(where))
    return values.at[spots[0]].set(low).at[spots[1]].set(high)


def block_scale(stream_key, extent, cuts, low, top_value):
    factor_of, own = 1.0, jax.random.fold_in(stream_key, 6)
    for axis_at, blocks in cuts:
        heights = jnp.exp(jax.random.uniform(jax.random.fold_in(own, axis_at), (blocks,), jnp.float32, low / len(cuts), top_value / len(cuts)))
        factor_of = factor_of * jnp.repeat(heights, extent[axis_at] // blocks).reshape([-1 if axis == axis_at else 1 for axis in range(len(extent))])
    return factor_of


def gaussian(own_key, dims, width, reach, shards=(), dtype=jnp.bfloat16):
    result = jax.random.normal(own_key, dims, jnp.float32) * width
    if len(shards) > 0:
        result = block_scale(own_key, dims, shards, -0.22, 0.18) * result
    return jnp.clip(result, min=-reach, max=reach).astype(dtype)


def setup_inputs(seed: int = 0) -> dict:
    key_list = jax.random.split(jax.random.key(seed), 8)
    primal_image = jnp.clip(1.0 * jax.random.uniform(key_list[0], (NCH, NY, NX), jnp.float32) ** block_scale(key_list[0], (NCH, NY, NX), ((0, 4), (1, 64)), -0.2, 0.2), 0.0, 1.0)
    dual_coef = gaussian(key_list[1], (4, NCH, NY // 2, NX // 2), 1.0, 6.0, ((1, 4), (2, 64)), jnp.float32)
    l21_weight = jnp.clip(jnp.exp(math.log(16.0) - 2.0794415 * jax.random.uniform(key_list[2], (4, NY // 2, NX // 2), jnp.float32) ** block_scale(key_list[2], (4, NY // 2, NX // 2), ((1, 64),), -0.2, 0.2)), 2.0, 16.0)
    visibilities = gaussian(key_list[3], (NCH, NVIS), 1.0, 6.0, ((0, 64), (1, 4)))
    tile_index = touch_ends(jax.random.randint(key_list[4], (NCH, NVIS), 0, NTILE), jax.random.fold_in(key_list[4], 1), 0, NTILE - 1).astype(jnp.int32)
    kernel_values = gaussian(key_list[5], (NCH, NVIS, 128), 1.0, 6.0, ((0, 64), (1, 4)))
    kernel_pattern = touch_ends((jax.random.randint(key_list[6], (NCH, NVIS, 128), 0, 2) < 1).astype(jnp.int32), jax.random.fold_in(key_list[6], 1), 0, 1)
    return dict(primal_image=primal_image, dual_coef=dual_coef, l21_weight=l21_weight, visibilities=visibilities, tile_index=tile_index, kernel_values=kernel_values, kernel_pattern=kernel_pattern)


FILTER_LOW = [0.23037781330885523, 0.7148465705525415, 0.6308807679295904, -0.02798376941698385, -0.18703481171888114, 0.030841381835986965, 0.032883011666982945, -0.010597401784997278]
FILTER_HIGH = [(-1.0) ** offset * FILTER_LOW[7 - offset] for offset in range(8)]
STEP_PRIMAL = 0.5
STEP_DUAL = 1.0

def pad_axis(array, which_axis, pad_before, pad_after):
    widths = [(0, 0)] * array.ndim
    widths[which_axis] = (pad_before, pad_after)
    return jnp.pad(array, widths)

def analyze(extended, filters, which_axis):
    out_count = (extended.shape[which_axis] - 7) // 2
    summed = 0.0
    for offset in range(8):
        summed = summed + filters[offset] * lax.slice_in_dim(extended, offset, offset + 2 * out_count - 1, 2, which_axis)
    return summed

def synthesize(extended, filters, which_axis):
    out_count = extended.shape[which_axis] - 4
    even_rows = 0.0
    odd_rows = 0.0
    for pair_index in range(4):
        even_rows = even_rows + filters[2 * pair_index + 1] * lax.slice_in_dim(extended, 3 - pair_index, 3 - pair_index + out_count, 1, which_axis)
        odd_rows = odd_rows + filters[2 * pair_index] * lax.slice_in_dim(extended, 4 - pair_index, 4 - pair_index + out_count, 1, which_axis)
    paired = jnp.stack([even_rows, odd_rows], axis=which_axis + 1)
    new_shape = list(even_rows.shape)
    new_shape[which_axis] = 2 * out_count
    return paired.reshape(new_shape)

def columns_forward(rows_band):
    extended = pad_axis(rows_band, 2, 3, 4)
    return (analyze(extended, FILTER_LOW, 2), analyze(extended, FILTER_HIGH, 2))

def forward_wavelet(rows_extended):
    rows_low = analyze(rows_extended, FILTER_LOW, 1)
    rows_high = analyze(rows_extended, FILTER_HIGH, 1)
    band_ll, band_lh = columns_forward(rows_low)
    band_hl, band_hh = columns_forward(rows_high)
    return jnp.stack([band_ll, band_lh, band_hl, band_hh], axis=0)

def columns_adjoint(coef):
    low_rows = synthesize(pad_axis(coef[0], 2, 2, 2), FILTER_LOW, 2) + synthesize(pad_axis(coef[1], 2, 2, 2), FILTER_HIGH, 2)
    high_rows = synthesize(pad_axis(coef[2], 2, 2, 2), FILTER_LOW, 2) + synthesize(pad_axis(coef[3], 2, 2, 2), FILTER_HIGH, 2)
    return jnp.stack([low_rows, high_rows], axis=0)

def rows_adjoint(row_bands_extended):
    return synthesize(row_bands_extended[0], FILTER_LOW, 1) + synthesize(row_bands_extended[1], FILTER_HIGH, 1)

def back_project(visibilities, tile_index, kernel_values, kernel_pattern):
    quarter = NX // N_CHAN
    kernels = kernel_values.astype(jnp.float32) * kernel_pattern.astype(jnp.float32)
    flat_vis = visibilities.reshape(NCH * N_CHAN, VIS_DEV)
    flat_tiles = tile_index.reshape(NCH * N_CHAN, VIS_DEV)
    flat_kernels = kernels.reshape(NCH * N_CHAN, VIS_DEV, 128)

    def one_block(operands):
        values, tiles_here, kernels_here = operands
        contrib = values.astype(jnp.float32)[:, None] * kernels_here
        gridded = jax.ops.segment_sum(contrib, tiles_here, num_segments=NTILE)
        return gridded.reshape(NY, quarter)
    blocks = lax.map(one_block, (flat_vis, flat_tiles, flat_kernels))
    blocks = blocks.reshape(NCH, N_CHAN, NY, quarter)
    return jnp.transpose(blocks, (0, 2, 1, 3)).reshape(NCH, NY, NX)

def reference(primal_image, dual_coef, l21_weight, visibilities, tile_index, kernel_values, kernel_pattern):
    back = back_project(visibilities, tile_index, kernel_values, kernel_pattern)
    row_bands = columns_adjoint(dual_coef)
    synth = rows_adjoint(pad_axis(row_bands, 2, 2, 2))
    image_next = jnp.maximum(primal_image - STEP_PRIMAL * (synth + back), 0.0)
    change = 2.0 * image_next - primal_image
    update = dual_coef + STEP_DUAL * forward_wavelet(pad_axis(change, 1, 3, 4))
    radius = jnp.sqrt(lax.optimization_barrier(jnp.sum(update * update, axis=1)))
    factor = l21_weight / jnp.maximum(radius, l21_weight)
    dual_next = update * factor[:, None]
    return (image_next, dual_next)
```

```python
import jax
import jax.numpy as jnp
import ml_dtypes
import numpy as np
from jax import lax
from jax.experimental import pallas as pl
from jax.experimental.pallas import tpu as pltpu
from jax.sharding import PartitionSpec as P

FILTER_LOW = [
    0.23037781330885523,
    0.7148465705525415,
    0.6308807679295904,
    -0.02798376941698385,
    -0.18703481171888114,
    0.030841381835986965,
    0.032883011666982945,
    -0.010597401784997278,
]
FILTER_HIGH = [(-1.0) ** offset * FILTER_LOW[7 - offset] for offset in range(8)]
STEP_PRIMAL = 0.5
STEP_DUAL = 1.0
LANES = 128
VMEM_BYTES = 48 * 1024 * 1024


def taps(filters, offset):
    table = np.asarray(filters, np.float64)
    valid = (offset >= 0) & (offset < 8)
    return np.where(valid, table[np.clip(offset, 0, 7)], 0.0)


def split_constant(matrix):
    matrix = matrix.astype(np.float32)
    high = matrix.astype(ml_dtypes.bfloat16)
    low = (matrix - high.astype(np.float32)).astype(ml_dtypes.bfloat16)
    return jnp.asarray(np.stack([high, low]))


def split(values):
    high = values.astype(jnp.bfloat16)
    low = (values - high.astype(jnp.float32)).astype(jnp.bfloat16)
    return high, low


def product(a, b):
    return jnp.dot(a, b, preferred_element_type=jnp.float32)


def product_left(matrix, values):
    high, low = split(values)
    return product(matrix[0], high) + product(matrix[0], low) + product(matrix[1], high)


def synthesis_rows(channels, rows):
    halves = rows // 2
    pixel = np.arange(rows)[:, None]
    blocks = []
    for first, count in ((0, halves), (-2, 2), (halves, 2)):
        coef = first + np.arange(count)[None, :]
        for filters in (FILTER_LOW, FILTER_HIGH):
            blocks.append(np.kron(np.eye(channels), taps(filters, pixel - 2 * coef + 3)))
    own_low, own_high, top_low, top_high, bottom_low, bottom_high = blocks
    return np.concatenate([own_low, own_high, top_low, bottom_low, top_high, bottom_high], axis=1)


def synthesis_columns():
    coef = np.arange(3 * LANES)[:, None] - LANES
    pixel = np.arange(2 * LANES)[None, :]
    return np.concatenate(
        [taps(filters, pixel - 2 * coef + 3) for filters in (FILTER_LOW, FILTER_HIGH)], axis=0
    )


def analysis_rows(channels, rows):
    coef = np.arange(rows // 2)[:, None]
    own, halo = [], []
    for filters in (FILTER_LOW, FILTER_HIGH):
        pixel = np.arange(rows)[None, :]
        own.append(np.kron(np.eye(channels), taps(filters, pixel - 2 * coef + 3)))
        sides = []
        for pixel_at in (-3, -2, -1, rows, rows + 1, rows + 2):
            column = taps(filters, pixel_at - 2 * coef + 3)
            sides.append(np.kron(np.eye(channels), column))
        halo.append(np.concatenate(sides, axis=1))
    return np.concatenate(own, axis=0), np.concatenate(halo, axis=0)


def analysis_columns():
    pixel = np.arange(4 * LANES)[:, None] - LANES
    coef = np.arange(LANES)[None, :]
    return np.concatenate(
        [taps(filters, pixel - 2 * coef + 3) for filters in (FILTER_LOW, FILTER_HIGH)], axis=1
    )


def border_rows(channels, rows):
    ends = (0, 1, 2, rows - 3, rows - 2, rows - 1)
    picked = [np.kron(np.eye(channels), np.arange(rows)[None, :] == row) for row in ends]
    return np.concatenate(picked, axis=0).astype(ml_dtypes.bfloat16)


def back_kernel(vis_ref, tile_ref, kernel_ref, pattern_ref, out_ref, cells_ref):
    count = tile_ref.shape[1]
    rows_here = out_ref.shape[0]
    step = 512

    @pl.when(pl.program_id(0) == 0)
    def _():
        def fill(index, carry):
            at = pl.multiple_of(index * step, step)
            tile = tile_ref[:, pl.ds(at, step)] & 3
            lane_tile = jnp.transpose(jnp.broadcast_to(tile, (LANES, step)))
            kept = jnp.where(pattern_ref[pl.ds(at, step), :] != 0, lane_tile, 4)
            values = kernel_ref[pl.ds(at, step), :].astype(jnp.float32)
            for part in range(4):
                cells_ref[pl.ds(at, step), part * LANES : (part + 1) * LANES] = jnp.where(
                    kept == part, values, 0.0
                ).astype(jnp.bfloat16)
            return carry

        lax.fori_loop(0, count // step, fill, 0)

    row = pl.program_id(0) * rows_here + lax.broadcasted_iota(jnp.int32, (rows_here, step), 0)

    def add(index, total):
        at = pl.multiple_of(index * step, step)
        here = (tile_ref[:, pl.ds(at, step)] >> 2) == row
        values = vis_ref[:, pl.ds(at, step)].astype(jnp.float32)
        spread = jnp.where(here, values, 0.0).astype(jnp.bfloat16)
        out_ref[...] += product(spread, cells_ref[pl.ds(at, step), :])
        return total

    out_ref[...] = jnp.zeros_like(out_ref)
    lax.fori_loop(0, count // step, add, 0)


def back_project(vis, tile, kernels, pattern, rows_all, quarter):
    count = tile.shape[1]
    block = 256
    whole = lambda i: (0, 0)
    return pl.pallas_call(
        back_kernel,
        grid=(rows_all // block,),
        in_specs=[
            pl.BlockSpec((1, count), whole),
            pl.BlockSpec((1, count), whole),
            pl.BlockSpec((count, LANES), whole),
            pl.BlockSpec((count, LANES), whole),
        ],
        out_specs=pl.BlockSpec((block, quarter), lambda i: (i, 0)),
        out_shape=jax.ShapeDtypeStruct((rows_all, quarter), jnp.float32),
        scratch_shapes=[pltpu.VMEM((count, quarter), jnp.bfloat16)],
        compiler_params=pltpu.CompilerParams(vmem_limit_bytes=VMEM_BYTES),
        cost_estimate=pl.CostEstimate(
            flops=2 * rows_all * count * quarter, bytes_accessed=6 << 20, transcendentals=0
        ),
        name="back_project",
    )(vis, tile, kernels, pattern)


def synthesis_kernel(dual_ref, top_ref, bottom_ref, primal_ref, rows_ref, columns_ref, out_ref, mid_ref):
    tiles = dual_ref.shape[2] // LANES
    for kind in range(2):
        for at in range(0, tiles, 2):
            lanes = slice(at * LANES, (at + 2) * LANES)
            stacked = jnp.concatenate(
                [
                    dual_ref[kind, :, lanes],
                    dual_ref[kind + 2, :, lanes],
                    top_ref[kind, :, lanes],
                    bottom_ref[kind, :, lanes],
                    top_ref[kind + 2, :, lanes],
                    bottom_ref[kind + 2, :, lanes],
                ],
                axis=0,
            )
            high, low = split(product_left(rows_ref, stacked))
            mid_ref[kind, 0, :, lanes] = high
            mid_ref[kind, 1, :, lanes] = low
    for at in range(tiles):
        first, last = max(at - 1, 0), min(at + 2, tiles)
        lanes = slice(first * LANES, last * LANES)
        total = 0.0
        for kind in range(2):
            base = (3 * kind + first - at + 1) * LANES
            part = slice(base, base + (last - first) * LANES)
            total = total + product(mid_ref[kind, 0, :, lanes], columns_ref[0, part, :])
            total = total + product(mid_ref[kind, 1, :, lanes], columns_ref[0, part, :])
            total = total + product(mid_ref[kind, 0, :, lanes], columns_ref[1, part, :])
        pixels = slice(2 * at * LANES, 2 * (at + 1) * LANES)
        out_ref[:, pixels] = primal_ref[:, pixels] - STEP_PRIMAL * total


def synthesize(dual, top, bottom, primal, channels, rows):
    pixels, columns = primal.shape
    return pl.pallas_call(
        synthesis_kernel,
        out_shape=jax.ShapeDtypeStruct(primal.shape, jnp.float32),
        scratch_shapes=[pltpu.VMEM((2, 2, pixels, columns // 2), jnp.bfloat16)],
        compiler_params=pltpu.CompilerParams(vmem_limit_bytes=VMEM_BYTES),
        cost_estimate=pl.CostEstimate(
            flops=4 << 30, bytes_accessed=8 << 20, transcendentals=0
        ),
        name="synthesis",
    )(
        dual,
        top,
        bottom,
        primal,
        split_constant(synthesis_rows(channels, rows)),
        split_constant(synthesis_columns()),
    )


def image_kernel(base_ref, back_ref, primal_ref, pick_ref, image_ref, top_ref, bottom_ref):
    image = jnp.maximum(base_ref[...] - STEP_PRIMAL * back_ref[0], 0.0)
    image_ref[...] = image
    high, low = split(2.0 * image - primal_ref[...])
    sides = product(pick_ref[...], high) + product(pick_ref[...], low)
    half = sides.shape[0] // 2
    top_ref[...] = sides[:half]
    bottom_ref[...] = sides[half:]


def update_image(base, back, primal, channels, rows):
    parts, pixels, quarter = back.shape
    block = pl.BlockSpec((pixels, quarter), lambda i: (0, i))
    side = pl.BlockSpec((3 * channels, quarter), lambda i: (0, i))
    side_shape = jax.ShapeDtypeStruct((3 * channels, parts * quarter), jnp.float32)
    pick = border_rows(channels, rows)
    return pl.pallas_call(
        image_kernel,
        grid=(parts,),
        in_specs=[
            block,
            pl.BlockSpec((1, pixels, quarter), lambda i: (i, 0, 0)),
            block,
            pl.BlockSpec(pick.shape, lambda i: (0, 0)),
        ],
        out_specs=[block, side, side],
        out_shape=[jax.ShapeDtypeStruct(base.shape, jnp.float32), side_shape, side_shape],
        compiler_params=pltpu.CompilerParams(vmem_limit_bytes=VMEM_BYTES),
        cost_estimate=pl.CostEstimate(flops=4 << 20, bytes_accessed=8 << 20, transcendentals=0),
        name="update_image",
    )(base, back, primal, jnp.asarray(pick))


def analysis_kernel(
    image_ref, primal_ref, above_ref, below_ref, dual_ref, own_ref, halo_ref, columns_ref,
    update_ref, squares_ref, mid_ref,
):
    tiles = image_ref.shape[1] // LANES
    half = mid_ref.shape[1] // 2
    for at in range(0, tiles, 2):
        lanes = slice(at * LANES, (at + 2) * LANES)
        change = 2.0 * image_ref[:, lanes] - primal_ref[:, lanes]
        sides = jnp.concatenate([above_ref[:, lanes], below_ref[:, lanes]], axis=0)
        banded = product_left(own_ref, change) + product_left(halo_ref, sides)
        high, low = split(banded)
        mid_ref[0, :, lanes] = high
        mid_ref[1, :, lanes] = low
    for at in range(0, tiles, 2):
        first, last = max(at - 1, 0), min(at + 3, tiles)
        lanes = slice(first * LANES, last * LANES)
        part = slice((first - at + 1) * LANES, (last - at + 1) * LANES)
        both = product(mid_ref[0, :, lanes], columns_ref[0, part, :])
        both = both + product(mid_ref[1, :, lanes], columns_ref[0, part, :])
        both = both + product(mid_ref[0, :, lanes], columns_ref[1, part, :])
        out = slice(at // 2 * LANES, (at // 2 + 1) * LANES)
        for band in range(4):
            rows = slice(band // 2 * half, (band // 2 + 1) * half)
            cols = slice(band % 2 * LANES, (band % 2 + 1) * LANES)
            update = dual_ref[band, :, out] + STEP_DUAL * both[rows, cols]
            update_ref[band, :, out] = update
            squares = update * update
            squares_ref[band, :, out] = jnp.sum(
                squares.reshape(-1, squares_ref.shape[1], LANES), axis=0
            )


def analyze(image, primal, above, below, dual, channels, rows):
    own, halo = analysis_rows(channels, rows)
    return pl.pallas_call(
        analysis_kernel,
        out_shape=[
            jax.ShapeDtypeStruct(dual.shape, jnp.float32),
            jax.ShapeDtypeStruct((4, rows // 2, dual.shape[2]), jnp.float32),
        ],
        scratch_shapes=[pltpu.VMEM((2,) + image.shape, jnp.bfloat16)],
        compiler_params=pltpu.CompilerParams(vmem_limit_bytes=VMEM_BYTES),
        cost_estimate=pl.CostEstimate(flops=4 << 30, bytes_accessed=10 << 20, transcendentals=0),
        name="analysis",
    )(
        image,
        primal,
        above,
        below,
        dual,
        split_constant(own),
        split_constant(halo),
        split_constant(analysis_columns()),
    )


def project_kernel(update_ref, weight_ref, one_ref, two_ref, three_ref, four_ref, out_ref):
    total = (one_ref[0] + two_ref[0]) + (three_ref[0] + four_ref[0])
    weight = weight_ref[0]
    factor = weight / jnp.maximum(jnp.sqrt(total), weight)
    count = factor.shape[0]
    for channel in range(update_ref.shape[1] // count):
        rows = slice(channel * count, (channel + 1) * count)
        out_ref[0, rows, :] = update_ref[0, rows, :] * factor


def project(update, weight, sums):
    bands, pixels, columns = update.shape
    wide = pl.BlockSpec((1, pixels, columns), lambda i: (i, 0, 0))
    narrow = pl.BlockSpec((1, weight.shape[1], columns), lambda i: (i, 0, 0))
    return pl.pallas_call(
        project_kernel,
        grid=(bands,),
        in_specs=[wide] + [narrow] * 5,
        out_specs=wide,
        out_shape=jax.ShapeDtypeStruct(update.shape, jnp.float32),
        compiler_params=pltpu.CompilerParams(vmem_limit_bytes=VMEM_BYTES),
        cost_estimate=pl.CostEstimate(flops=4 << 20, bytes_accessed=5 << 20, transcendentals=0),
        name="project",
    )(update, weight, *sums)


def shards(
    primal_image, dual_coef, l21_weight, visibilities, tile_index, kernel_values, kernel_pattern
):
    facets, groups = lax.axis_size("fac"), lax.axis_size("chan")
    channels, rows, columns = primal_image.shape
    quarter = columns // groups
    forward = [(i, i + 1) for i in range(facets - 1)]
    backward = [(b, a) for a, b in forward]

    halves = rows // 2
    top = lax.ppermute(
        dual_coef[:, :, halves - 2 :].reshape(4, 2 * channels, columns // 2), "fac", forward
    )
    bottom = lax.ppermute(
        dual_coef[:, :, :2].reshape(4, 2 * channels, columns // 2), "fac", backward
    )

    gridded = back_project(
        visibilities, tile_index, kernel_values[0], kernel_pattern[0], rows * facets, quarter
    )
    by_facet = lax.all_to_all(
        gridded.reshape(facets, rows, quarter), "fac", split_axis=0, concat_axis=0, tiled=True
    )
    back = lax.all_to_all(by_facet, "chan", split_axis=0, concat_axis=0, tiled=True)
    back = back.reshape(groups, channels * rows, quarter)

    primal = primal_image.reshape(channels * rows, columns)
    dual = dual_coef.reshape(4, channels * halves, columns // 2)
    base = synthesize(dual, top, bottom, primal, channels, rows)
    image, first, last = update_image(base, back, primal, channels, rows)
    above = lax.ppermute(last, "fac", forward)
    below = lax.ppermute(first, "fac", backward)
    update, squares = analyze(image, primal, above, below, dual, channels, rows)
    sums = [squares]
    for step in range(1, groups):
        pairs = [(i, (i + step) % groups) for i in range(groups)]
        sums.append(lax.ppermute(squares, "chan", pairs))
    dual_next = project(update, l21_weight, sums)
    return (image.reshape(primal_image.shape), dual_next.reshape(dual_coef.shape))


def solution(mesh):
    in_specs = (
        P("chan", "fac", None),
        P(None, "chan", "fac", None),
        P(None, "fac", None),
        P("fac", "chan"),
        P("fac", "chan"),
        P("fac", "chan", None),
        P("fac", "chan", None),
    )
    out_specs = (P("chan", "fac", None), P(None, "chan", "fac", None))
    return jax.shard_map(shards, mesh=mesh, in_specs=in_specs, out_specs=out_specs, check_vma=False)
```

```python
import functools

import jax
import jax.numpy as jnp
import ml_dtypes
import numpy as np
from jax import lax
from jax.experimental import pallas as pl
from jax.experimental.pallas import tpu as pltpu
from jax.sharding import PartitionSpec as P

FILTER_LOW = [
    0.23037781330885523,
    0.7148465705525415,
    0.6308807679295904,
    -0.02798376941698385,
    -0.18703481171888114,
    0.030841381835986965,
    0.032883011666982945,
    -0.010597401784997278,
]
FILTER_HIGH = [(-1.0) ** offset * FILTER_LOW[7 - offset] for offset in range(8)]
STEP_PRIMAL = 0.5
STEP_DUAL = 1.0
LANES = 128
VMEM_BYTES = 24 * 1024 * 1024
BACK_VMEM_BYTES = 60 * 1024 * 1024
PARTS = 4


def taps(filters, offset):
    table = np.asarray(filters, np.float64)
    valid = (offset >= 0) & (offset < 8)
    return np.where(valid, table[np.clip(offset, 0, 7)], 0.0)


def split_constant(matrix):
    matrix = matrix.astype(np.float32)
    high = matrix.astype(ml_dtypes.bfloat16)
    low = (matrix - high.astype(np.float32)).astype(ml_dtypes.bfloat16)
    return jnp.asarray(np.stack([high, low]))


def split(values):
    high = values.astype(jnp.bfloat16)
    low = (values - high.astype(jnp.float32)).astype(jnp.bfloat16)
    return high, low


def product(a, b):
    return jnp.dot(a, b, preferred_element_type=jnp.float32)


def product_left(matrix, values):
    high, low = split(values)
    return product(matrix[0], high) + product(matrix[0], low) + product(matrix[1], high)


def part_rows(rows):
    half = rows // 2
    a = [row if row < half // 2 else row + half for row in range(half)]
    b = [row + half if row < half // 2 else row for row in range(half)]
    return np.array(a), np.array(b)


def synthesis_rows(channels, rows):
    coef = np.arange(rows // 2)[None, :]
    a, b = part_rows(rows)
    sides = (-3, -2, -1, rows, rows + 1, rows + 2)
    blocks = []
    for filters in (FILTER_LOW, FILTER_HIGH):
        parts = [np.kron(np.eye(channels), taps(filters, p[:, None] - 2 * coef + 3)) for p in (a, b)]
        parts += [np.kron(np.eye(channels), taps(filters, row - 2 * coef + 3)) for row in sides]
        blocks.append(np.concatenate(parts, axis=0))
    return np.concatenate(blocks, axis=1)


def synthesis_columns():
    coef = np.arange(3 * LANES)[:, None] - LANES
    pixel = np.arange(2 * LANES)[None, :]
    return np.concatenate(
        [taps(filters, pixel - 2 * coef + 3) for filters in (FILTER_LOW, FILTER_HIGH)], axis=0
    )


def analysis_rows(channels, rows):
    coef = np.arange(rows // 2)[:, None]
    a, b = part_rows(rows)
    sides = (-3, -2, -1, rows, rows + 1, rows + 2)
    bands = []
    for filters in (FILTER_LOW, FILTER_HIGH):
        parts = [np.kron(np.eye(channels), taps(filters, p[None, :] - 2 * coef + 3)) for p in (a, b)]
        parts += [np.kron(np.eye(channels), taps(filters, row - 2 * coef + 3)) for row in sides]
        bands.append(np.concatenate(parts, axis=1))
    return np.concatenate(bands, axis=0)


def analysis_columns():
    pixel = np.arange(4 * LANES)[:, None] - LANES
    coef = np.arange(LANES)[None, :]
    return np.concatenate(
        [taps(filters, pixel - 2 * coef + 3) for filters in (FILTER_LOW, FILTER_HIGH)], axis=1
    )


def border_rows(channels, rows):
    a, _ = part_rows(rows)
    ends = (0, 1, 2, rows - 3, rows - 2, rows - 1)
    picked = [np.kron(np.eye(channels), a[None, :] == row) for row in ends]
    return np.concatenate(picked, axis=0).astype(ml_dtypes.bfloat16)


def back_kernel(
    vis_ref, tile_ref, kernel_hbm, pattern_hbm, out_hbm,
    kernel_ref, pattern_ref, cells_ref, out_ref, sems, out_sems, *, rows,
):
    count = tile_ref.shape[1]
    step = 512
    steps = count // step
    half = rows // 2
    parts = out_ref.shape[0]
    slots = out_ref.shape[1]

    def copies(index):
        at = pl.ds(index * step, step)
        return (
            pltpu.make_async_copy(pattern_hbm.at[at, :], pattern_ref.at[at, :], sems.at[0, index]),
            pltpu.make_async_copy(kernel_hbm.at[at, :], kernel_ref.at[at, :], sems.at[1, index]),
        )

    def copy_out(part):
        return pltpu.make_async_copy(
            out_ref.at[part], out_hbm.at[pl.ds(part * slots, slots), :], out_sems.at[part]
        )

    for index in range(steps):
        for copy in copies(index):
            copy.start()

    tile = tile_ref[...]
    row = tile >> 2
    within = row & (rows - 1)
    in_b = ((within >> 2) ^ (within >> 3)) & 1
    place = (row - within) + half * in_b + (within & (half - 1))
    iota = lax.broadcasted_iota(jnp.int32, (slots, step), 0)
    values = vis_ref[...].astype(jnp.float32)

    for part in range(parts):
        total = None
        for index in range(steps):
            at = slice(index * step, (index + 1) * step)
            if part == 0:
                for copy in copies(index):
                    copy.wait()
                lane_tile = jnp.transpose(jnp.broadcast_to(tile[:, at] & 3, (LANES, step)))
                kept = jnp.where(pattern_ref[at, :] != 0, lane_tile, 4)
                kernels = kernel_ref[at, :].astype(jnp.float32)
                for column in range(4):
                    cells_ref[at, column * LANES : (column + 1) * LANES] = jnp.where(
                        kept == column, kernels, 0.0
                    ).astype(jnp.bfloat16)
            here = place[:, at] - part * slots == iota
            spread = jnp.where(here, values[:, at], 0.0).astype(jnp.bfloat16)
            term = product(spread, cells_ref[at, :])
            total = term if total is None else total + term
        out_ref[part] = total
        copy_out(part).start()
    for part in range(parts):
        copy_out(part).wait()


def back_project(vis, tile, kernels, pattern, rows, facets, quarter):
    count = tile.shape[1]
    parts = PARTS
    slots = rows * facets // parts
    vmem = pl.BlockSpec(memory_space=pltpu.VMEM)
    hbm = pl.BlockSpec(memory_space=pl.ANY)
    return pl.pallas_call(
        functools.partial(back_kernel, rows=rows),
        in_specs=[vmem, vmem, hbm, hbm],
        out_specs=hbm,
        out_shape=jax.ShapeDtypeStruct((rows * facets, quarter), jnp.float32),
        scratch_shapes=[
            pltpu.VMEM((count, LANES), kernels.dtype),
            pltpu.VMEM((count, LANES), pattern.dtype),
            pltpu.VMEM((count, quarter), jnp.bfloat16),
            pltpu.VMEM((parts, slots, quarter), jnp.float32),
            pltpu.SemaphoreType.DMA((2, count // 512)),
            pltpu.SemaphoreType.DMA((parts,)),
        ],
        compiler_params=pltpu.CompilerParams(vmem_limit_bytes=BACK_VMEM_BYTES),
        cost_estimate=pl.CostEstimate(
            flops=2 * rows * facets * count * quarter, bytes_accessed=6 << 20, transcendentals=0
        ),
        name="back_project",
    )(vis, tile, kernels, pattern)


def pick_part(natural, part):
    half = natural.shape[2]
    first = lax.broadcasted_iota(jnp.int32, natural[:, 0].shape, 1) < half // 2
    one, two = (natural[:, 0], natural[:, 1]) if part == 0 else (natural[:, 1], natural[:, 0])
    return jnp.where(first, one, two).reshape(-1, natural.shape[3])


def synthesis_kernel(dual_ref, primal_ref, rows_ref, columns_ref, a_ref, b_ref, above_ref, below_ref, mid_ref):
    tiles = dual_ref.shape[2] // LANES
    for kind in range(2):
        for at in range(0, tiles, 2):
            lanes = slice(at * LANES, (at + 2) * LANES)
            stacked = jnp.concatenate([dual_ref[kind, :, lanes], dual_ref[kind + 2, :, lanes]], axis=0)
            high, low = split(product_left(rows_ref, stacked))
            mid_ref[kind, 0, :, lanes] = high
            mid_ref[kind, 1, :, lanes] = low
    half = a_ref.shape[0]
    side = above_ref.shape[0]
    for at in range(tiles):
        first, last = max(at - 1, 0), min(at + 2, tiles)
        lanes = slice(first * LANES, last * LANES)
        total = 0.0
        for kind in range(2):
            base = (3 * kind + first - at + 1) * LANES
            part = slice(base, base + (last - first) * LANES)
            total = total + product(mid_ref[kind, 0, :, lanes], columns_ref[0, part, :])
            total = total + product(mid_ref[kind, 1, :, lanes], columns_ref[0, part, :])
            total = total + product(mid_ref[kind, 0, :, lanes], columns_ref[1, part, :])
        pixels = slice(2 * at * LANES, 2 * (at + 1) * LANES)
        primal = primal_ref[:, :, :, pixels]
        a_ref[:, pixels] = pick_part(primal, 0) - STEP_PRIMAL * total[:half]
        b_ref[:, pixels] = pick_part(primal, 1) - STEP_PRIMAL * total[half : 2 * half]
        above_ref[:, pixels] = total[2 * half : 2 * half + side]
        below_ref[:, pixels] = total[2 * half + side :]


def synthesize(dual, primal):
    channels, _, half, columns = primal.shape
    part = jax.ShapeDtypeStruct((channels * half, columns), jnp.float32)
    side = jax.ShapeDtypeStruct((3 * channels, columns), jnp.float32)
    rows = split_constant(synthesis_rows(channels, 2 * half))
    return pl.pallas_call(
        synthesis_kernel,
        out_shape=[part, part, side, side],
        scratch_shapes=[pltpu.VMEM((2, 2, rows.shape[1], columns // 2), jnp.bfloat16)],
        compiler_params=pltpu.CompilerParams(vmem_limit_bytes=VMEM_BYTES),
        cost_estimate=pl.CostEstimate(flops=8 << 30, bytes_accessed=8 << 20, transcendentals=0),
        name="synthesis",
    )(dual, primal, rows, split_constant(synthesis_columns()))


def border_kernel(
    me_ref, base_ref, own_ref, one_ref, two_ref, three_ref, primal_ref, pick_ref,
    image_ref, first_ref, last_ref,
):
    base = base_ref[...]
    for step, back_ref in enumerate((own_ref, one_ref, two_ref, three_ref)):

        @pl.when(pl.program_id(0) == step)
        def _(back_ref=back_ref):
            back = back_ref[...].reshape(base.shape)
            image_ref[...] = jnp.maximum(base - STEP_PRIMAL * back, 0.0)

    high, low = split(2.0 * image_ref[...] - pick_part(primal_ref[...], 0))
    picked = product(pick_ref[...], high) + product(pick_ref[...], low)
    half = picked.shape[0] // 2
    first_ref[...] = picked[:half]
    last_ref[...] = picked[half:]


def sides_kernel(base_ref, above_ref, below_ref, place_ref, out_ref):
    high, low = split(jnp.concatenate([above_ref[...], below_ref[...]], axis=0))
    added = product(place_ref[...], high) + product(place_ref[...], low)
    out_ref[...] = base_ref[...] - STEP_PRIMAL * added


def add_sides(base, above, below):
    pixels, columns = base.shape
    channels = above.shape[0] // 3
    place = border_rows(channels, 2 * pixels // channels).T
    return pl.pallas_call(
        sides_kernel,
        out_shape=jax.ShapeDtypeStruct(base.shape, jnp.float32),
        compiler_params=pltpu.CompilerParams(vmem_limit_bytes=VMEM_BYTES),
        cost_estimate=pl.CostEstimate(flops=1 << 30, bytes_accessed=3 << 20, transcendentals=0),
        name="add_sides",
    )(base, above, below, jnp.asarray(place))


def own_part(parts, part):
    _, channels, _, half, quarter = parts.shape
    return pl.BlockSpec((1, channels, 1, half, quarter), lambda i, me: (me[0], 0, part, 0, 0))


def update_border(me, base, parts, backs, primal):
    pixels, columns = base.shape
    channels, _, half, _ = primal.shape
    groups = parts.shape[0]
    quarter = columns // groups
    pick = border_rows(channels, 2 * half)
    block = pl.BlockSpec((pixels, quarter), lambda i, me: (0, i ^ me[0]))
    side = pl.BlockSpec((3 * channels, quarter), lambda i, me: (0, i ^ me[0]))
    whole = lambda i, me: (0, 0)
    side_shape = jax.ShapeDtypeStruct((3 * channels, columns), jnp.float32)
    return pl.pallas_call(
        border_kernel,
        grid_spec=pltpu.PrefetchScalarGridSpec(
            num_scalar_prefetch=1,
            grid=(groups,),
            in_specs=[block, own_part(parts, 0)]
            + [pl.BlockSpec((pixels, quarter), whole)] * len(backs)
            + [
                pl.BlockSpec((channels, 2, half, quarter), lambda i, me: (0, 0, 0, i ^ me[0])),
                pl.BlockSpec(pick.shape, whole),
            ],
            out_specs=[block, side, side],
        ),
        out_shape=[jax.ShapeDtypeStruct(base.shape, jnp.float32), side_shape, side_shape],
        compiler_params=pltpu.CompilerParams(vmem_limit_bytes=VMEM_BYTES),
        cost_estimate=pl.CostEstimate(flops=4 << 20, bytes_accessed=8 << 20, transcendentals=0),
        name="update_border",
    )(me, base, parts, *backs, primal, jnp.asarray(pick))


def finish_kernel(
    me_ref, image_a_ref, base_b_ref, own_ref, one_ref, two_ref, three_ref, primal_ref, above_ref,
    below_ref, dual_ref, rows_ref, columns_ref, image_ref, update_ref, squares_ref, mid_ref, back_ref,
):
    step = pl.program_id(0)
    channels, _, half, width = image_ref.shape
    edge = LANES
    columns = mid_ref.shape[2] - 2 * edge
    blocks = columns // width

    @pl.when(step == 0)
    def _():
        zeros = jnp.zeros(mid_ref.shape[:2] + (edge,), mid_ref.dtype)
        mid_ref[:, :, :edge] = zeros
        mid_ref[:, :, edge + columns :] = zeros

    for part, part_ref in enumerate((own_ref, one_ref, two_ref, three_ref)):

        @pl.when((step ^ me_ref[0]) == part)
        def _(part_ref=part_ref):
            back_ref[...] = part_ref[...].reshape(back_ref.shape)

    @pl.when(step < blocks)
    def _():
        image_b = jnp.maximum(base_b_ref[...] - STEP_PRIMAL * back_ref[...], 0.0)
        image_a = image_a_ref[...]
        wide_a = image_a.reshape(channels, half, width)
        wide_b = image_b.reshape(channels, half, width)
        first = lax.broadcasted_iota(jnp.int32, wide_a.shape, 1) < half // 2
        image_ref[:, 0] = jnp.where(first, wide_a, wide_b)
        image_ref[:, 1] = jnp.where(first, wide_b, wide_a)
        primal = primal_ref[...]
        stacked = jnp.concatenate(
            [
                2.0 * image_a - pick_part(primal, 0),
                2.0 * image_b - pick_part(primal, 1),
                above_ref[...],
                below_ref[...],
            ],
            axis=0,
        )
        high, low = split(product_left(rows_ref, stacked))
        at = pl.ds(pl.multiple_of(edge + step * width, LANES), width)
        mid_ref[0, :, at] = high
        mid_ref[1, :, at] = low

    rows = mid_ref.shape[1] // 2

    @pl.when(step > 0)
    def _():
        for block in range(width // (2 * LANES)):
            start = pl.multiple_of((step - 1) * width + block * 2 * LANES, LANES)
            high = mid_ref[0, :, pl.ds(start, 4 * LANES)]
            low = mid_ref[1, :, pl.ds(start, 4 * LANES)]
            both = product(high, columns_ref[0]) + product(low, columns_ref[0])
            both = both + product(high, columns_ref[1])
            out = slice(block * LANES, (block + 1) * LANES)
            for band in range(4):
                here = slice(band // 2 * rows, (band // 2 + 1) * rows)
                cols = slice(band % 2 * LANES, (band % 2 + 1) * LANES)
                update = dual_ref[band, :, out] + STEP_DUAL * both[here, cols]
                update_ref[band, :, out] = update
                squares = update * update
                squares_ref[band, :, out] = jnp.sum(squares.reshape(-1, half, LANES), axis=0)


def finish(me, image_a, base_b, parts, core_b, far_b, primal, above, below, dual):
    channels, _, half, columns = primal.shape
    rows = split_constant(analysis_rows(channels, 2 * half))
    taps_across = split_constant(analysis_columns())
    blocks = parts.shape[0]
    width = columns // blocks
    pixels = channels * half
    now = lambda i, me: (0, jnp.minimum(i, blocks - 1))
    now4 = lambda i, me: (0, 0, 0, jnp.minimum(i, blocks - 1))
    before = lambda i, me: (0, 0, jnp.maximum(i - 1, 0))
    whole3 = lambda i, me: (0, 0, 0)
    part = pl.BlockSpec((pixels, width), now)
    side = pl.BlockSpec((3 * channels, width), now)
    return pl.pallas_call(
        finish_kernel,
        grid_spec=pltpu.PrefetchScalarGridSpec(
            num_scalar_prefetch=1,
            grid=(blocks + 1,),
            in_specs=[
                part,
                part,
                own_part(parts, 1),
                pl.BlockSpec((1, pixels, width), whole3),
                pl.BlockSpec((1, pixels, width), whole3),
                pl.BlockSpec((1, pixels, width), lambda i, me: (1, 0, 0)),
                pl.BlockSpec((channels, 2, half, width), now4),
                side,
                side,
                pl.BlockSpec((4, pixels, width // 2), before),
                pl.BlockSpec(rows.shape, whole3),
                pl.BlockSpec(taps_across.shape, whole3),
            ],
            out_specs=[
                pl.BlockSpec((channels, 2, half, width), now4),
                pl.BlockSpec((4, pixels, width // 2), before),
                pl.BlockSpec((4, half, width // 2), before),
            ],
            scratch_shapes=[
                pltpu.VMEM((2, rows.shape[1], columns + 2 * LANES), jnp.bfloat16),
                pltpu.VMEM((pixels, width), jnp.float32),
            ],
        ),
        out_shape=[
            jax.ShapeDtypeStruct(primal.shape, jnp.float32),
            jax.ShapeDtypeStruct(dual.shape, jnp.float32),
            jax.ShapeDtypeStruct((4, half, dual.shape[2]), jnp.float32),
        ],
        compiler_params=pltpu.CompilerParams(vmem_limit_bytes=VMEM_BYTES),
        cost_estimate=pl.CostEstimate(flops=4 << 30, bytes_accessed=12 << 20, transcendentals=0),
        name="finish",
    )(me, image_a, base_b, parts, core_b, far_b, far_b, primal, above, below, dual, rows, taps_across)


def project_kernel(update_ref, weight_ref, one_ref, two_ref, three_ref, four_ref, out_ref):
    total = (one_ref[0] + two_ref[0]) + (three_ref[0] + four_ref[0])
    weight = weight_ref[0]
    factor = weight / jnp.maximum(jnp.sqrt(total), weight)
    count = factor.shape[0]
    for channel in range(update_ref.shape[1] // count):
        rows = slice(channel * count, (channel + 1) * count)
        out_ref[0, rows, :] = update_ref[0, rows, :] * factor


def project(update, weight, sums):
    bands, pixels, columns = update.shape
    wide = pl.BlockSpec((1, pixels, columns), lambda i: (i, 0, 0))
    narrow = pl.BlockSpec((1, weight.shape[1], columns), lambda i: (i, 0, 0))
    return pl.pallas_call(
        project_kernel,
        grid=(bands,),
        in_specs=[wide] + [narrow] * 5,
        out_specs=wide,
        out_shape=jax.ShapeDtypeStruct(update.shape, jnp.float32),
        compiler_params=pltpu.CompilerParams(vmem_limit_bytes=VMEM_BYTES),
        cost_estimate=pl.CostEstimate(flops=4 << 20, bytes_accessed=5 << 20, transcendentals=0),
        name="project",
    )(update, weight, *sums)


def shards(
    primal_image, dual_coef, l21_weight, visibilities, tile_index, kernel_values, kernel_pattern
):
    facets, groups = lax.axis_size("fac"), lax.axis_size("chan")
    channels, rows, columns = primal_image.shape
    quarter = columns // groups
    half = rows // 2
    forward = [(i, i + 1) for i in range(facets - 1)]
    backward = [(b, a) for a, b in forward]
    me = lax.axis_index("chan")
    primal = primal_image.reshape(channels, 2, half, columns)
    dual = dual_coef.reshape(4, channels * half, columns // 2)

    grid = back_project(
        visibilities, tile_index, kernel_values[0], kernel_pattern[0], rows, facets, quarter
    )
    by_facet = lax.all_to_all(
        grid.reshape(facets, rows, quarter), "fac", split_axis=0, concat_axis=0, tiled=True
    )
    dual_here, _ = lax.optimization_barrier((dual, grid))
    base_a, base_b, to_above, to_below = synthesize(dual_here, primal)
    from_above = lax.ppermute(to_below, "fac", forward)
    from_below = lax.ppermute(to_above, "fac", backward)
    by_facet, from_above, from_below = lax.optimization_barrier((by_facet, from_above, from_below))
    base_a = add_sides(base_a, from_above, from_below)

    parts = by_facet.reshape(groups, channels, 2, half, quarter)

    def piece(part, step):
        return lax.dynamic_index_in_dim(parts[:, :, part], me ^ step, 0, False).reshape(-1, quarter)

    def pairs(step):
        return [(i, i ^ step) for i in range(groups)]

    sent_a = [piece(0, step) for step in (1, 2, 3)]
    sent_b = jnp.stack([piece(1, 1), piece(1, 3)])
    kept_b = piece(1, 2)
    sent_a, sent_b, kept_b = lax.optimization_barrier((sent_a, sent_b, kept_b))
    backs_a = [lax.ppermute(sent_a[step - 1], "chan", pairs(step)) for step in (1, 2, 3)]
    core_b = lax.ppermute(sent_b, "chan", pairs(1))
    far_b = lax.ppermute(jnp.stack([kept_b, core_b[1]]), "chan", pairs(2))
    me = me.astype(jnp.int32).reshape(1)
    image_a, first, last = update_border(me, base_a, parts, backs_a, primal)
    above = lax.ppermute(last, "fac", forward)
    below = lax.ppermute(first, "fac", backward)
    image, update, squares = finish(
        me, image_a, base_b, parts, core_b, far_b, primal, above, below, dual
    )
    sums = [squares]
    for step in range(1, groups):
        pairs = [(i, i ^ step) for i in range(groups)]
        sums.append(lax.ppermute(squares, "chan", pairs))
    dual_next = project(update, l21_weight, sums)
    return (image.reshape(primal_image.shape), dual_next.reshape(dual_coef.shape))


def solution(mesh):
    in_specs = (
        P("chan", "fac", None),
        P(None, "chan", "fac", None),
        P(None, "fac", None),
        P("fac", "chan"),
        P("fac", "chan"),
        P("fac", "chan", None),
        P("fac", "chan", None),
    )
    out_specs = (P("chan", "fac", None), P(None, "chan", "fac", None))
    return jax.shard_map(shards, mesh=mesh, in_specs=in_specs, out_specs=out_specs, check_vma=False)
```

```python
import functools

import jax
import jax.numpy as jnp
import ml_dtypes
import numpy as np
from jax import lax
from jax.experimental import pallas as pl
from jax.experimental.pallas import tpu as pltpu
from jax.sharding import PartitionSpec as P

FILTER_LOW = [
    0.23037781330885523,
    0.7148465705525415,
    0.6308807679295904,
    -0.02798376941698385,
    -0.18703481171888114,
    0.030841381835986965,
    0.032883011666982945,
    -0.010597401784997278,
]
FILTER_HIGH = [(-1.0) ** offset * FILTER_LOW[7 - offset] for offset in range(8)]
STEP_PRIMAL = 0.5
STEP_DUAL = 1.0
LANES = 128
VMEM_BYTES = 24 * 1024 * 1024
BACK_VMEM_BYTES = 60 * 1024 * 1024
PARTS = 4
RING = 8


def taps(filters, offset):
    table = np.asarray(filters, np.float64)
    valid = (offset >= 0) & (offset < 8)
    return np.where(valid, table[np.clip(offset, 0, 7)], 0.0)


def split_constant(matrix):
    matrix = matrix.astype(np.float32)
    high = matrix.astype(ml_dtypes.bfloat16)
    low = (matrix - high.astype(np.float32)).astype(ml_dtypes.bfloat16)
    return jnp.asarray(np.stack([high, low]))


def split(values):
    high = values.astype(jnp.bfloat16)
    low = (values - high.astype(jnp.float32)).astype(jnp.bfloat16)
    return high, low


def product(a, b):
    return jnp.dot(a, b, preferred_element_type=jnp.float32)


def product_left(matrix, values):
    high, low = split(values)
    return product(matrix[0], high) + product(matrix[0], low) + product(matrix[1], high)


def part_rows(rows):
    half = rows // 2
    a = [row if row < half // 2 else row + half for row in range(half)]
    b = [row + half if row < half // 2 else row for row in range(half)]
    return np.array(a), np.array(b)


def synthesis_rows(channels, rows):
    coef = np.arange(rows // 2)[None, :]
    a, b = part_rows(rows)
    sides = (-3, -2, -1, rows, rows + 1, rows + 2)
    blocks = []
    for filters in (FILTER_LOW, FILTER_HIGH):
        parts = [np.kron(np.eye(channels), taps(filters, p[:, None] - 2 * coef + 3)) for p in (a, b)]
        parts += [np.kron(np.eye(channels), taps(filters, row - 2 * coef + 3)) for row in sides]
        blocks.append(np.concatenate(parts, axis=0))
    return np.concatenate(blocks, axis=1)


def synthesis_columns():
    coef = np.arange(3 * LANES)[:, None] - LANES
    pixel = np.arange(2 * LANES)[None, :]
    return np.concatenate(
        [taps(filters, pixel - 2 * coef + 3) for filters in (FILTER_LOW, FILTER_HIGH)], axis=0
    )


def analysis_rows(channels, rows):
    coef = np.arange(rows // 2)[:, None]
    a, b = part_rows(rows)
    sides = (-3, -2, -1, rows, rows + 1, rows + 2)
    bands = []
    for filters in (FILTER_LOW, FILTER_HIGH):
        parts = [np.kron(np.eye(channels), taps(filters, p[None, :] - 2 * coef + 3)) for p in (a, b)]
        parts += [np.kron(np.eye(channels), taps(filters, row - 2 * coef + 3)) for row in sides]
        bands.append(np.concatenate(parts, axis=1))
    return np.concatenate(bands, axis=0)


def analysis_columns():
    pixel = np.arange(4 * LANES)[:, None] - LANES
    coef = np.arange(LANES)[None, :]
    return np.concatenate(
        [taps(filters, pixel - 2 * coef + 3) for filters in (FILTER_LOW, FILTER_HIGH)], axis=1
    )


def border_rows(channels, rows):
    a, _ = part_rows(rows)
    ends = (0, 1, 2, rows - 3, rows - 2, rows - 1)
    picked = [np.kron(np.eye(channels), a[None, :] == row) for row in ends]
    return np.concatenate(picked, axis=0).astype(ml_dtypes.bfloat16)


def back_kernel(
    vis_ref, tile_ref, kernel_hbm, pattern_hbm, out_hbm,
    kernel_ref, pattern_ref, cells_ref, out_ref, sems, out_sems, *, rows,
):
    count = tile_ref.shape[1]
    step = 1024
    steps = count // step
    half = rows // 2
    parts = out_ref.shape[0]
    slots = out_ref.shape[1]

    def copies(index):
        at = pl.ds(index * step, step)
        return (
            pltpu.make_async_copy(pattern_hbm.at[at, :], pattern_ref.at[at, :], sems.at[0, index]),
            pltpu.make_async_copy(kernel_hbm.at[at, :], kernel_ref.at[at, :], sems.at[1, index]),
        )

    def copy_out(part):
        return pltpu.make_async_copy(
            out_ref.at[part], out_hbm.at[pl.ds(part * slots, slots), :], out_sems.at[part]
        )

    for index in range(steps):
        for copy in copies(index):
            copy.start()

    tile = tile_ref[...]
    row = tile >> 2
    within = row & (rows - 1)
    in_b = ((within >> 2) ^ (within >> 3)) & 1
    place = (row - within) + half * in_b + (within & (half - 1))
    iota = lax.broadcasted_iota(jnp.int32, (slots, step), 0).astype(jnp.float32).astype(jnp.bfloat16)
    values = vis_ref[...]
    zero = jnp.zeros((), jnp.bfloat16)

    for part in range(parts):
        total = None
        for index in range(steps):
            at = slice(index * step, (index + 1) * step)
            if part == 0:
                for copy in copies(index):
                    copy.wait()
                lane_tile = jnp.transpose(jnp.broadcast_to(tile[:, at] & 3, (LANES, step)))
                kept = jnp.where(pattern_ref[at, :] != 0, lane_tile, 4)
                kept = kept.astype(jnp.float32).astype(jnp.bfloat16)
                kernels = kernel_ref[at, :]
                for column in range(4):
                    cells_ref[at, column * LANES : (column + 1) * LANES] = jnp.where(
                        kept == column, kernels, zero
                    )
            local = place[:, at] - part * slots
            local = jnp.where((local >= 0) & (local < slots), local, -1)
            local = local.astype(jnp.float32).astype(jnp.bfloat16)
            spread = jnp.where(local == iota, values[:, at], zero)
            term = product(spread, cells_ref[at, :])
            total = term if total is None else total + term
        out_ref[part] = total
        copy_out(part).start()
    for part in range(parts):
        copy_out(part).wait()


def back_project(vis, tile, kernels, pattern, rows, facets, quarter):
    count = tile.shape[1]
    parts = PARTS
    slots = rows * facets // parts
    vmem = pl.BlockSpec(memory_space=pltpu.VMEM)
    hbm = pl.BlockSpec(memory_space=pl.ANY)
    return pl.pallas_call(
        functools.partial(back_kernel, rows=rows),
        in_specs=[vmem, vmem, hbm, hbm],
        out_specs=hbm,
        out_shape=jax.ShapeDtypeStruct((rows * facets, quarter), jnp.float32),
        scratch_shapes=[
            pltpu.VMEM((count, LANES), kernels.dtype),
            pltpu.VMEM((count, LANES), pattern.dtype),
            pltpu.VMEM((count, quarter), jnp.bfloat16),
            pltpu.VMEM((parts, slots, quarter), jnp.float32),
            pltpu.SemaphoreType.DMA((2, count // 1024)),
            pltpu.SemaphoreType.DMA((parts,)),
        ],
        compiler_params=pltpu.CompilerParams(vmem_limit_bytes=BACK_VMEM_BYTES),
        cost_estimate=pl.CostEstimate(
            flops=2 * rows * facets * count * quarter, bytes_accessed=6 << 20, transcendentals=0
        ),
        name="back_project",
    )(vis, tile, kernels, pattern)


def pick_part(natural, part):
    half = natural.shape[2]
    first = lax.broadcasted_iota(jnp.int32, natural[:, 0].shape, 1) < half // 2
    one, two = (natural[:, 0], natural[:, 1]) if part == 0 else (natural[:, 1], natural[:, 0])
    return jnp.where(first, one, two).reshape(-1, natural.shape[3])


def synthesis_kernel(dual_ref, primal_ref, rows_ref, columns_ref, a_ref, b_ref, above_ref, below_ref, mid_ref):
    tiles = dual_ref.shape[2] // LANES
    for kind in range(2):
        for at in range(0, tiles, 2):
            lanes = slice(at * LANES, (at + 2) * LANES)
            stacked = jnp.concatenate([dual_ref[kind, :, lanes], dual_ref[kind + 2, :, lanes]], axis=0)
            high, low = split(product_left(rows_ref, stacked))
            mid_ref[kind, 0, :, lanes] = high
            mid_ref[kind, 1, :, lanes] = low
    half = a_ref.shape[0]
    side = above_ref.shape[0]
    for at in range(tiles):
        first, last = max(at - 1, 0), min(at + 2, tiles)
        lanes = slice(first * LANES, last * LANES)
        total = 0.0
        for kind in range(2):
            base = (3 * kind + first - at + 1) * LANES
            part = slice(base, base + (last - first) * LANES)
            total = total + product(mid_ref[kind, 0, :, lanes], columns_ref[0, part, :])
            total = total + product(mid_ref[kind, 1, :, lanes], columns_ref[0, part, :])
            total = total + product(mid_ref[kind, 0, :, lanes], columns_ref[1, part, :])
        pixels = slice(2 * at * LANES, 2 * (at + 1) * LANES)
        primal = primal_ref[:, :, :, pixels]
        a_ref[:, pixels] = pick_part(primal, 0) - STEP_PRIMAL * total[:half]
        b_ref[:, pixels] = pick_part(primal, 1) - STEP_PRIMAL * total[half : 2 * half]
        above_ref[:, pixels] = total[2 * half : 2 * half + side]
        below_ref[:, pixels] = total[2 * half + side :]


def synthesize(dual, primal):
    channels, _, half, columns = primal.shape
    part = jax.ShapeDtypeStruct((channels * half, columns), jnp.float32)
    side = jax.ShapeDtypeStruct((3 * channels, columns), jnp.float32)
    rows = split_constant(synthesis_rows(channels, 2 * half))
    return pl.pallas_call(
        synthesis_kernel,
        out_shape=[part, part, side, side],
        scratch_shapes=[pltpu.VMEM((2, 2, rows.shape[1], columns // 2), jnp.bfloat16)],
        compiler_params=pltpu.CompilerParams(vmem_limit_bytes=VMEM_BYTES),
        cost_estimate=pl.CostEstimate(flops=8 << 30, bytes_accessed=8 << 20, transcendentals=0),
        name="synthesis",
    )(dual, primal, rows, split_constant(synthesis_columns()))


def own_part(parts, part):
    _, channels, _, half, quarter = parts.shape
    return pl.BlockSpec((1, channels, 1, half, quarter), lambda i, me: (me[0], 0, part, 0, 0))


def sides_kernel(base_ref, above_ref, below_ref, place_ref, out_ref):
    high, low = split(jnp.concatenate([above_ref[...], below_ref[...]], axis=0))
    added = product(place_ref[...], high) + product(place_ref[...], low)
    out_ref[...] = base_ref[...] - STEP_PRIMAL * added


def add_sides(base, above, below):
    pixels, columns = base.shape
    channels = above.shape[0] // 3
    place = border_rows(channels, 2 * pixels // channels).T
    return pl.pallas_call(
        sides_kernel,
        out_shape=jax.ShapeDtypeStruct(base.shape, jnp.float32),
        compiler_params=pltpu.CompilerParams(vmem_limit_bytes=VMEM_BYTES),
        cost_estimate=pl.CostEstimate(flops=40 << 30, bytes_accessed=3 << 20, transcendentals=0),
        name="add_sides",
    )(base, above, below, jnp.asarray(place))


def border_sum_kernel(me_ref, base_ref, own_ref, one_ref, two_ref, three_ref, out_ref):
    for step, back_ref in enumerate((own_ref, one_ref, two_ref, three_ref)):

        @pl.when(pl.program_id(0) == step)
        def _(back_ref=back_ref):
            out_ref[...] = base_ref[...] - STEP_PRIMAL * back_ref[...].reshape(base_ref.shape)


def border_sum(me, base, parts, backs):
    pixels, columns = base.shape
    groups = parts.shape[0]
    quarter = columns // groups
    block = pl.BlockSpec((pixels, quarter), lambda i, me: (0, i ^ me[0]))
    whole = lambda i, me: (0, 0)
    return pl.pallas_call(
        border_sum_kernel,
        grid_spec=pltpu.PrefetchScalarGridSpec(
            num_scalar_prefetch=1,
            grid=(groups,),
            in_specs=[block, own_part(parts, 0)]
            + [pl.BlockSpec((pixels, quarter), whole)] * len(backs),
            out_specs=block,
        ),
        out_shape=jax.ShapeDtypeStruct(base.shape, jnp.float32),
        compiler_params=pltpu.CompilerParams(vmem_limit_bytes=VMEM_BYTES),
        cost_estimate=pl.CostEstimate(flops=20 << 30, bytes_accessed=3 << 20, transcendentals=0),
        name="border_sum",
    )(me, base, parts, *backs)


def border_kernel(
    base_ref, above_ref, below_ref, primal_ref, pick_ref, place_ref, image_ref, first_ref, last_ref
):
    high, low = split(jnp.concatenate([above_ref[...], below_ref[...]], axis=0))
    added = product(place_ref[...], high) + product(place_ref[...], low)
    image = jnp.maximum(base_ref[...] - STEP_PRIMAL * added, 0.0)
    image_ref[...] = image
    high, low = split(2.0 * image - pick_part(primal_ref[...], 0))
    picked = product(pick_ref[...], high) + product(pick_ref[...], low)
    half = picked.shape[0] // 2
    first_ref[...] = picked[:half]
    last_ref[...] = picked[half:]


def update_border(base, sides, primal):
    pixels, columns = base.shape
    channels, _, half, _ = primal.shape
    blocks = 4
    width = columns // blocks
    pick = border_rows(channels, 2 * half)
    block = pl.BlockSpec((pixels, width), lambda i: (0, i))
    side = pl.BlockSpec((3 * channels, width), lambda i: (0, i))
    whole = lambda i: (0, 0)
    side_shape = jax.ShapeDtypeStruct((3 * channels, columns), jnp.float32)
    return pl.pallas_call(
        border_kernel,
        grid=(blocks,),
        in_specs=[
            block,
            side,
            side,
            pl.BlockSpec((channels, 2, half, width), lambda i: (0, 0, 0, i)),
            pl.BlockSpec(pick.shape, whole),
            pl.BlockSpec(pick.shape[::-1], whole),
        ],
        out_specs=[block, side, side],
        out_shape=[jax.ShapeDtypeStruct(base.shape, jnp.float32), side_shape, side_shape],
        compiler_params=pltpu.CompilerParams(vmem_limit_bytes=VMEM_BYTES),
        cost_estimate=pl.CostEstimate(flops=4 << 20, bytes_accessed=4 << 20, transcendentals=0),
        name="update_border",
    )(base, *sides, primal, jnp.asarray(pick), jnp.asarray(pick.T))


def finish_kernel(
    me_ref, image_a_ref, base_b_ref, own_ref, one_ref, two_ref, three_ref, primal_ref,
    dual_ref, rows_ref, columns_ref, image_ref, update_ref, mid_ref, back_ref,
):
    step = pl.program_id(0)
    channels, _, half, width = image_ref.shape
    edge = LANES
    columns = mid_ref.shape[2] - 2 * edge
    blocks = columns // width

    @pl.when(step == 0)
    def _():
        zeros = jnp.zeros(mid_ref.shape[:2] + (edge,), mid_ref.dtype)
        mid_ref[:, :, :edge] = zeros
        mid_ref[:, :, edge + columns :] = zeros

    for part, part_ref in enumerate((own_ref, one_ref, two_ref, three_ref)):

        @pl.when((step ^ me_ref[0]) == part)
        def _(part_ref=part_ref):
            back_ref[...] = part_ref[...].reshape(back_ref.shape)

    @pl.when(step < blocks)
    def _():
        image_b = jnp.maximum(base_b_ref[...] - STEP_PRIMAL * back_ref[...], 0.0)
        image_a = image_a_ref[...]
        wide_a = image_a.reshape(channels, half, width)
        wide_b = image_b.reshape(channels, half, width)
        first = lax.broadcasted_iota(jnp.int32, wide_a.shape, 1) < half // 2
        image_ref[:, 0] = jnp.where(first, wide_a, wide_b)
        image_ref[:, 1] = jnp.where(first, wide_b, wide_a)
        primal = primal_ref[...]
        stacked = jnp.concatenate(
            [
                2.0 * image_a - pick_part(primal, 0),
                2.0 * image_b - pick_part(primal, 1),
            ],
            axis=0,
        )
        high, low = split(product_left(rows_ref, stacked))
        at = pl.ds(pl.multiple_of(edge + step * width, LANES), width)
        mid_ref[0, :, at] = high
        mid_ref[1, :, at] = low

    rows = mid_ref.shape[1] // 2

    @pl.when(step > 0)
    def _():
        for block in range(width // (2 * LANES)):
            start = pl.multiple_of((step - 1) * width + block * 2 * LANES, LANES)
            high = mid_ref[0, :, pl.ds(start, 4 * LANES)]
            low = mid_ref[1, :, pl.ds(start, 4 * LANES)]
            both = product(high, columns_ref[0]) + product(low, columns_ref[0])
            both = both + product(high, columns_ref[1])
            out = slice(block * LANES, (block + 1) * LANES)
            for band in range(4):
                here = slice(band // 2 * rows, (band // 2 + 1) * rows)
                cols = slice(band % 2 * LANES, (band % 2 + 1) * LANES)
                update_ref[band, :, out] = dual_ref[band, :, out] + STEP_DUAL * both[here, cols]


def finish(me, image_a, base_b, parts, core_b, far_b, primal, dual):
    channels, _, half, columns = primal.shape
    rows = split_constant(analysis_rows(channels, 2 * half)[:, : 2 * channels * half])
    taps_across = split_constant(analysis_columns())
    blocks = parts.shape[0]
    width = columns // blocks
    pixels = channels * half
    now = lambda i, me: (0, jnp.minimum(i, blocks - 1))
    now4 = lambda i, me: (0, 0, 0, jnp.minimum(i, blocks - 1))
    before = lambda i, me: (0, 0, jnp.maximum(i - 1, 0))
    whole3 = lambda i, me: (0, 0, 0)
    part = pl.BlockSpec((pixels, width), now)
    return pl.pallas_call(
        finish_kernel,
        grid_spec=pltpu.PrefetchScalarGridSpec(
            num_scalar_prefetch=1,
            grid=(blocks + 1,),
            in_specs=[
                part,
                part,
                own_part(parts, 1),
                pl.BlockSpec((1, pixels, width), whole3),
                pl.BlockSpec((1, pixels, width), whole3),
                pl.BlockSpec((1, pixels, width), lambda i, me: (1, 0, 0)),
                pl.BlockSpec((channels, 2, half, width), now4),
                pl.BlockSpec((4, pixels, width // 2), before),
                pl.BlockSpec(rows.shape, whole3),
                pl.BlockSpec(taps_across.shape, whole3),
            ],
            out_specs=[
                pl.BlockSpec((channels, 2, half, width), now4),
                pl.BlockSpec((4, pixels, width // 2), before),
            ],
            scratch_shapes=[
                pltpu.VMEM((2, rows.shape[1], columns + 2 * LANES), jnp.bfloat16),
                pltpu.VMEM((pixels, width), jnp.float32),
            ],
        ),
        out_shape=[
            jax.ShapeDtypeStruct(primal.shape, jnp.float32),
            jax.ShapeDtypeStruct(dual.shape, jnp.float32),
        ],
        compiler_params=pltpu.CompilerParams(vmem_limit_bytes=VMEM_BYTES),
        cost_estimate=pl.CostEstimate(flops=4 << 30, bytes_accessed=12 << 20, transcendentals=0),
        name="finish",
    )(me, image_a, base_b, parts, core_b, far_b, far_b, primal, dual, rows, taps_across)


def halo_kernel(
    main_ref, above_ref, below_ref, rows_ref, columns_ref, update_ref, squares_ref, mid_ref
):
    step = pl.program_id(0)
    edge = LANES
    columns = above_ref.shape[1]
    _, _, width = update_ref.shape
    half = squares_ref.shape[1]
    count = mid_ref.shape[0] // 2

    @pl.when(step == 0)
    def _():
        zeros = jnp.zeros((2 * count, edge), mid_ref.dtype)
        mid_ref[:, :edge] = zeros
        mid_ref[:, edge + columns :] = zeros
        high, low = split(jnp.concatenate([above_ref[...], below_ref[...]], axis=0))
        mid_ref[:count, edge : edge + columns] = high
        mid_ref[count:, edge : edge + columns] = low

    rows = rows_ref.shape[1] // 2
    for block in range(width // LANES):
        start = pl.multiple_of(2 * (step * width + block * LANES), LANES)
        window = mid_ref[:, pl.ds(start, 4 * LANES)]
        once = product(window, columns_ref[0])
        across = once[:count] + once[count:] + product(window[:count], columns_ref[1])
        both = product_left(rows_ref, across)
        out = slice(block * LANES, (block + 1) * LANES)
        for band in range(4):
            here = slice(band // 2 * rows, (band // 2 + 1) * rows)
            cols = slice(band % 2 * LANES, (band % 2 + 1) * LANES)
            update = main_ref[band, :, out] + STEP_DUAL * both[here, cols]
            update_ref[band, :, out] = update
            squares = update * update
            squares_ref[band, :, out] = jnp.sum(squares.reshape(-1, half, LANES), axis=0)


def add_halo(main, above, below, half):
    _, pixels, columns = main.shape
    channels = pixels // half
    rows = split_constant(analysis_rows(channels, 2 * half)[:, 2 * pixels :])
    taps_across = split_constant(analysis_columns())
    blocks = 4
    wide = pl.BlockSpec((4, pixels, columns // blocks), lambda i: (0, 0, i))
    whole = lambda i: (0, 0)
    whole3 = lambda i: (0, 0, 0)
    return pl.pallas_call(
        halo_kernel,
        grid=(blocks,),
        in_specs=[
            wide,
            pl.BlockSpec(above.shape, whole),
            pl.BlockSpec(below.shape, whole),
            pl.BlockSpec(rows.shape, whole3),
            pl.BlockSpec(taps_across.shape, whole3),
        ],
        out_specs=[wide, pl.BlockSpec((4, half, columns // blocks), lambda i: (0, 0, i))],
        out_shape=[
            jax.ShapeDtypeStruct(main.shape, jnp.float32),
            jax.ShapeDtypeStruct((4, half, columns), jnp.float32),
        ],
        scratch_shapes=[pltpu.VMEM((4 * above.shape[0], above.shape[1] + 2 * LANES), jnp.bfloat16)],
        compiler_params=pltpu.CompilerParams(vmem_limit_bytes=VMEM_BYTES),
        cost_estimate=pl.CostEstimate(flops=1 << 30, bytes_accessed=5 << 20, transcendentals=0),
        name="add_halo",
    )(main, above, below, rows, taps_across)


def project_kernel(update_ref, weight_ref, sums_ref, out_ref):
    total = (sums_ref[0, 0] + sums_ref[1, 0]) + (sums_ref[2, 0] + sums_ref[3, 0])
    weight = weight_ref[0]
    factor = weight / jnp.maximum(jnp.sqrt(total), weight)
    count = factor.shape[0]
    for channel in range(update_ref.shape[1] // count):
        rows = slice(channel * count, (channel + 1) * count)
        out_ref[0, rows, :] = update_ref[0, rows, :] * factor


def project(update, weight, sums):
    bands, pixels, columns = update.shape
    half = weight.shape[1]
    wide = pl.BlockSpec((1, pixels, columns), lambda i: (i, 0, 0))
    return pl.pallas_call(
        project_kernel,
        grid=(bands,),
        in_specs=[
            wide,
            pl.BlockSpec((1, half, columns), lambda i: (i, 0, 0)),
            pl.BlockSpec((sums.shape[0], 1, half, columns), lambda i: (0, i, 0, 0)),
        ],
        out_specs=wide,
        out_shape=jax.ShapeDtypeStruct(update.shape, jnp.float32),
        compiler_params=pltpu.CompilerParams(vmem_limit_bytes=VMEM_BYTES),
        cost_estimate=pl.CostEstimate(flops=4 << 20, bytes_accessed=5 << 20, transcendentals=0),
        name="project",
    )(update, weight, sums)


def shards(
    primal_image, dual_coef, l21_weight, visibilities, tile_index, kernel_values, kernel_pattern
):
    facets, groups = lax.axis_size("fac"), lax.axis_size("chan")
    channels, rows, columns = primal_image.shape
    quarter = columns // groups
    half = rows // 2
    forward = [(i, i + 1) for i in range(facets - 1)]
    backward = [(b, a) for a, b in forward]
    me = lax.axis_index("chan")
    primal = primal_image.reshape(channels, 2, half, columns)
    dual = dual_coef.reshape(4, channels * half, columns // 2)

    grid = back_project(
        visibilities, tile_index, kernel_values[0], kernel_pattern[0], rows, facets, quarter
    )
    by_facet = lax.all_to_all(
        grid.reshape(facets, rows, quarter), "fac", split_axis=0, concat_axis=0, tiled=True
    )
    dual_here, _ = lax.optimization_barrier((dual, grid))
    base_a, base_b, to_above, to_below = synthesize(dual_here, primal)
    near = [pair for pair in forward if pair[1] % RING != 0]
    far = [pair for pair in forward if pair[1] % RING == 0]
    turned = lambda those: [(b, a) for a, b in those]
    far_sides = [lax.ppermute(to_below, "fac", far), lax.ppermute(to_above, "fac", turned(far))]
    by_facet, to_above, to_below = lax.optimization_barrier((by_facet, to_above, to_below))
    sides = [lax.ppermute(to_below, "fac", near), lax.ppermute(to_above, "fac", turned(near))]
    parts = by_facet.reshape(groups, channels, 2, half, quarter)

    def piece(part, step):
        return lax.dynamic_index_in_dim(parts[:, :, part], me ^ step, 0, False).reshape(-1, quarter)

    def pairs(step):
        return [(i, i ^ step) for i in range(groups)]

    sent_a = [piece(0, step) for step in (1, 2, 3)]
    sent_b = jnp.stack([piece(1, 1), piece(1, 3)])
    kept_b = piece(1, 2)
    sent_a, sent_b, kept_b = lax.optimization_barrier((sent_a, sent_b, kept_b))
    backs_a = [lax.ppermute(sent_a[step - 1], "chan", pairs(step)) for step in (1, 2, 3)]
    core_b = lax.ppermute(sent_b, "chan", pairs(1))
    far_b = lax.ppermute(jnp.stack([kept_b, core_b[1]]), "chan", pairs(2))
    me = me.astype(jnp.int32).reshape(1)
    image_a, first, last = update_border(
        border_sum(me, add_sides(base_a, *far_sides), parts, backs_a), sides, primal
    )
    above = lax.ppermute(last, "fac", forward)
    below = lax.ppermute(first, "fac", backward)
    image, main = finish(me, image_a, base_b, parts, core_b, far_b, primal, dual)
    update, squares = add_halo(main, above, below, half)
    sums = lax.all_gather(squares, "chan")
    dual_next = project(update, l21_weight, sums)
    return (image.reshape(primal_image.shape), dual_next.reshape(dual_coef.shape))


def solution(mesh):
    in_specs = (
        P("chan", "fac", None),
        P(None, "chan", "fac", None),
        P(None, "fac", None),
        P("fac", "chan"),
        P("fac", "chan"),
        P("fac", "chan", None),
        P("fac", "chan", None),
    )
    out_specs = (P("chan", "fac", None), P(None, "chan", "fac", None))
    return jax.shard_map(shards, mesh=mesh, in_specs=in_specs, out_specs=out_specs, check_vma=False)
```

```python
import functools

import jax
import jax.numpy as jnp
import ml_dtypes
import numpy as np
from jax import lax
from jax.experimental import pallas as pl
from jax.experimental.pallas import tpu as pltpu
from jax.sharding import PartitionSpec as P

FILTER_LOW = [
    0.23037781330885523,
    0.7148465705525415,
    0.6308807679295904,
    -0.02798376941698385,
    -0.18703481171888114,
    0.030841381835986965,
    0.032883011666982945,
    -0.010597401784997278,
]
FILTER_HIGH = [(-1.0) ** offset * FILTER_LOW[7 - offset] for offset in range(8)]
STEP_PRIMAL = 0.5
STEP_DUAL = 1.0
LANES = 128
VMEM_BYTES = 24 * 1024 * 1024
BACK_VMEM_BYTES = 60 * 1024 * 1024
PARTS = 4
RING = 8


def taps(filters, offset):
    table = np.asarray(filters, np.float64)
    valid = (offset >= 0) & (offset < 8)
    return np.where(valid, table[np.clip(offset, 0, 7)], 0.0)


def split_constant(matrix):
    matrix = matrix.astype(np.float32)
    high = matrix.astype(ml_dtypes.bfloat16)
    low = (matrix - high.astype(np.float32)).astype(ml_dtypes.bfloat16)
    return jnp.asarray(np.stack([high, low]))


def split(values):
    high = values.astype(jnp.bfloat16)
    low = (values - high.astype(jnp.float32)).astype(jnp.bfloat16)
    return high, low


def product(a, b):
    return jnp.dot(a, b, preferred_element_type=jnp.float32)


def product_left(matrix, values):
    high, low = split(values)
    return product(matrix[0], high) + product(matrix[0], low) + product(matrix[1], high)


def part_rows(rows):
    half = rows // 2
    a = [row if row < half // 2 else row + half for row in range(half)]
    b = [row + half if row < half // 2 else row for row in range(half)]
    return np.array(a), np.array(b)


def synthesis_rows(channels, rows):
    coef = np.arange(rows // 2)[None, :]
    a, b = part_rows(rows)
    sides = (-3, -2, -1, rows, rows + 1, rows + 2)
    blocks = []
    for filters in (FILTER_LOW, FILTER_HIGH):
        parts = [np.kron(np.eye(channels), taps(filters, p[:, None] - 2 * coef + 3)) for p in (a, b)]
        parts += [np.kron(np.eye(channels), taps(filters, row - 2 * coef + 3)) for row in sides]
        blocks.append(np.concatenate(parts, axis=0))
    return np.concatenate(blocks, axis=1)


def synthesis_columns():
    coef = np.arange(3 * LANES)[:, None] - LANES
    pixel = np.arange(2 * LANES)[None, :]
    return np.concatenate(
        [taps(filters, pixel - 2 * coef + 3) for filters in (FILTER_LOW, FILTER_HIGH)], axis=0
    )


def analysis_rows(channels, rows):
    coef = np.arange(rows // 2)[:, None]
    a, b = part_rows(rows)
    sides = (-3, -2, -1, rows, rows + 1, rows + 2)
    bands = []
    for filters in (FILTER_LOW, FILTER_HIGH):
        parts = [np.kron(np.eye(channels), taps(filters, p[None, :] - 2 * coef + 3)) for p in (a, b)]
        parts += [np.kron(np.eye(channels), taps(filters, row - 2 * coef + 3)) for row in sides]
        bands.append(np.concatenate(parts, axis=1))
    return np.concatenate(bands, axis=0)


def analysis_columns():
    pixel = np.arange(4 * LANES)[:, None] - LANES
    coef = np.arange(LANES)[None, :]
    return np.concatenate(
        [taps(filters, pixel - 2 * coef + 3) for filters in (FILTER_LOW, FILTER_HIGH)], axis=1
    )


def border_rows(channels, rows):
    a, _ = part_rows(rows)
    ends = (0, 1, 2, rows - 3, rows - 2, rows - 1)
    picked = [np.kron(np.eye(channels), a[None, :] == row) for row in ends]
    return np.concatenate(picked, axis=0).astype(ml_dtypes.bfloat16)


def back_kernel(
    vis_ref, tile_ref, kernel_hbm, pattern_hbm, out_hbm,
    kernel_ref, pattern_ref, cells_ref, out_ref, sems, out_sems, *, rows,
):
    count = tile_ref.shape[1]
    step = 1024
    steps = count // step
    half = rows // 2
    parts = out_ref.shape[0]
    slots = out_ref.shape[1]

    def copies(index):
        at = pl.ds(index * step, step)
        return (
            pltpu.make_async_copy(pattern_hbm.at[at, :], pattern_ref.at[at, :], sems.at[0, index]),
            pltpu.make_async_copy(kernel_hbm.at[at, :], kernel_ref.at[at, :], sems.at[1, index]),
        )

    def copy_out(part):
        return pltpu.make_async_copy(
            out_ref.at[part], out_hbm.at[pl.ds(part * slots, slots), :], out_sems.at[part]
        )

    for index in range(steps):
        for copy in copies(index):
            copy.start()

    tile = tile_ref[...]
    row = tile >> 2
    within = row & (rows - 1)
    in_b = ((within >> 2) ^ (within >> 3)) & 1
    place = (row - within) + half * in_b + (within & (half - 1))
    iota = lax.broadcasted_iota(jnp.int32, (slots, step), 0).astype(jnp.float32).astype(jnp.bfloat16)
    values = vis_ref[...]
    zero = jnp.zeros((), jnp.bfloat16)

    for part in range(parts):
        total = None
        for index in range(steps):
            at = slice(index * step, (index + 1) * step)
            if part == 0:
                for copy in copies(index):
                    copy.wait()
                lane_tile = jnp.transpose(jnp.broadcast_to(tile[:, at] & 3, (LANES, step)))
                kept = jnp.where(pattern_ref[at, :] != 0, lane_tile, 4)
                kept = kept.astype(jnp.float32).astype(jnp.bfloat16)
                kernels = kernel_ref[at, :]
                for column in range(4):
                    cells_ref[at, column * LANES : (column + 1) * LANES] = jnp.where(
                        kept == column, kernels, zero
                    )
            local = place[:, at] - part * slots
            local = jnp.where((local >= 0) & (local < slots), local, -1)
            local = local.astype(jnp.float32).astype(jnp.bfloat16)
            spread = jnp.where(local == iota, values[:, at], zero)
            term = product(spread, cells_ref[at, :])
            total = term if total is None else total + term
        out_ref[part] = total
        copy_out(part).start()
    for part in range(parts):
        copy_out(part).wait()


def back_project(vis, tile, kernels, pattern, rows, facets, quarter):
    count = tile.shape[1]
    parts = PARTS
    slots = rows * facets // parts
    vmem = pl.BlockSpec(memory_space=pltpu.VMEM)
    hbm = pl.BlockSpec(memory_space=pl.ANY)
    return pl.pallas_call(
        functools.partial(back_kernel, rows=rows),
        in_specs=[vmem, vmem, hbm, hbm],
        out_specs=hbm,
        out_shape=jax.ShapeDtypeStruct((rows * facets, quarter), jnp.float32),
        scratch_shapes=[
            pltpu.VMEM((count, LANES), kernels.dtype),
            pltpu.VMEM((count, LANES), pattern.dtype),
            pltpu.VMEM((count, quarter), jnp.bfloat16),
            pltpu.VMEM((parts, slots, quarter), jnp.float32),
            pltpu.SemaphoreType.DMA((2, count // 1024)),
            pltpu.SemaphoreType.DMA((parts,)),
        ],
        compiler_params=pltpu.CompilerParams(vmem_limit_bytes=BACK_VMEM_BYTES),
        cost_estimate=pl.CostEstimate(
            flops=2 * rows * facets * count * quarter, bytes_accessed=6 << 20, transcendentals=0
        ),
        name="back_project",
    )(vis, tile, kernels, pattern)


def pick_part(natural, part):
    half = natural.shape[2]
    first = lax.broadcasted_iota(jnp.int32, natural[:, 0].shape, 1) < half // 2
    one, two = (natural[:, 0], natural[:, 1]) if part == 0 else (natural[:, 1], natural[:, 0])
    return jnp.where(first, one, two).reshape(-1, natural.shape[3])


def synthesis_kernel(dual_ref, primal_ref, rows_ref, columns_ref, a_ref, b_ref, above_ref, below_ref, mid_ref):
    tiles = dual_ref.shape[2] // LANES
    for kind in range(2):
        for at in range(0, tiles, 2):
            lanes = slice(at * LANES, (at + 2) * LANES)
            stacked = jnp.concatenate([dual_ref[kind, :, lanes], dual_ref[kind + 2, :, lanes]], axis=0)
            high, low = split(product_left(rows_ref, stacked))
            mid_ref[kind, 0, :, lanes] = high
            mid_ref[kind, 1, :, lanes] = low
    half = a_ref.shape[0]
    side = above_ref.shape[0]
    for at in range(tiles):
        first, last = max(at - 1, 0), min(at + 2, tiles)
        lanes = slice(first * LANES, last * LANES)
        total = 0.0
        for kind in range(2):
            base = (3 * kind + first - at + 1) * LANES
            part = slice(base, base + (last - first) * LANES)
            total = total + product(mid_ref[kind, 0, :, lanes], columns_ref[0, part, :])
            total = total + product(mid_ref[kind, 1, :, lanes], columns_ref[0, part, :])
            total = total + product(mid_ref[kind, 0, :, lanes], columns_ref[1, part, :])
        pixels = slice(2 * at * LANES, 2 * (at + 1) * LANES)
        primal = primal_ref[:, :, :, pixels]
        a_ref[:, pixels] = pick_part(primal, 0) - STEP_PRIMAL * total[:half]
        b_ref[:, pixels] = pick_part(primal, 1) - STEP_PRIMAL * total[half : 2 * half]
        above_ref[:, pixels] = total[2 * half : 2 * half + side]
        below_ref[:, pixels] = total[2 * half + side :]


def synthesize(dual, primal):
    channels, _, half, columns = primal.shape
    part = jax.ShapeDtypeStruct((channels * half, columns), jnp.float32)
    side = jax.ShapeDtypeStruct((3 * channels, columns), jnp.float32)
    rows = split_constant(synthesis_rows(channels, 2 * half))
    return pl.pallas_call(
        synthesis_kernel,
        out_shape=[part, part, side, side],
        scratch_shapes=[pltpu.VMEM((2, 2, rows.shape[1], columns // 2), jnp.bfloat16)],
        compiler_params=pltpu.CompilerParams(vmem_limit_bytes=VMEM_BYTES),
        cost_estimate=pl.CostEstimate(flops=8 << 30, bytes_accessed=8 << 20, transcendentals=0),
        name="synthesis",
    )(dual, primal, rows, split_constant(synthesis_columns()))


def own_part(parts, part):
    _, channels, _, half, quarter = parts.shape
    return pl.BlockSpec((1, channels, 1, half, quarter), lambda i, me: (me[0], 0, part, 0, 0))


def sides_kernel(base_ref, above_ref, below_ref, place_ref, out_ref):
    high, low = split(jnp.concatenate([above_ref[...], below_ref[...]], axis=0))
    added = product(place_ref[...], high) + product(place_ref[...], low)
    out_ref[...] = base_ref[...] - STEP_PRIMAL * added


def add_sides(base, above, below):
    pixels, columns = base.shape
    channels = above.shape[0] // 3
    place = border_rows(channels, 2 * pixels // channels).T
    return pl.pallas_call(
        sides_kernel,
        out_shape=jax.ShapeDtypeStruct(base.shape, jnp.float32),
        compiler_params=pltpu.CompilerParams(vmem_limit_bytes=VMEM_BYTES),
        cost_estimate=pl.CostEstimate(flops=40 << 30, bytes_accessed=3 << 20, transcendentals=0),
        name="add_sides",
    )(base, above, below, jnp.asarray(place))


def border_sum_kernel(me_ref, base_ref, own_ref, one_ref, two_ref, three_ref, out_ref):
    for step, back_ref in enumerate((own_ref, one_ref, two_ref, three_ref)):

        @pl.when(pl.program_id(0) == step)
        def _(back_ref=back_ref):
            out_ref[...] = base_ref[...] - STEP_PRIMAL * back_ref[...].reshape(base_ref.shape)


def border_sum(me, base, parts, backs):
    pixels, columns = base.shape
    groups = parts.shape[0]
    quarter = columns // groups
    block = pl.BlockSpec((pixels, quarter), lambda i, me: (0, i ^ me[0]))
    whole = lambda i, me: (0, 0)
    return pl.pallas_call(
        border_sum_kernel,
        grid_spec=pltpu.PrefetchScalarGridSpec(
            num_scalar_prefetch=1,
            grid=(groups,),
            in_specs=[block, own_part(parts, 0)]
            + [pl.BlockSpec((pixels, quarter), whole)] * len(backs),
            out_specs=block,
        ),
        out_shape=jax.ShapeDtypeStruct(base.shape, jnp.float32),
        compiler_params=pltpu.CompilerParams(vmem_limit_bytes=VMEM_BYTES),
        cost_estimate=pl.CostEstimate(flops=6 << 30, bytes_accessed=3 << 20, transcendentals=0),
        name="border_sum",
    )(me, base, parts, *backs)


def border_kernel(
    base_ref, above_ref, below_ref, primal_ref, pick_ref, place_ref, image_ref, first_ref, last_ref
):
    high, low = split(jnp.concatenate([above_ref[...], below_ref[...]], axis=0))
    added = product(place_ref[...], high) + product(place_ref[...], low)
    image = jnp.maximum(base_ref[...] - STEP_PRIMAL * added, 0.0)
    image_ref[...] = image
    high, low = split(2.0 * image - pick_part(primal_ref[...], 0))
    picked = product(pick_ref[...], high) + product(pick_ref[...], low)
    half = picked.shape[0] // 2
    first_ref[...] = picked[:half]
    last_ref[...] = picked[half:]


def update_border(base, sides, primal):
    pixels, columns = base.shape
    channels, _, half, _ = primal.shape
    blocks = 2
    width = columns // blocks
    pick = border_rows(channels, 2 * half)
    block = pl.BlockSpec((pixels, width), lambda i: (0, i))
    side = pl.BlockSpec((3 * channels, width), lambda i: (0, i))
    whole = lambda i: (0, 0)
    side_shape = jax.ShapeDtypeStruct((3 * channels, columns), jnp.float32)
    return pl.pallas_call(
        border_kernel,
        grid=(blocks,),
        in_specs=[
            block,
            side,
            side,
            pl.BlockSpec((channels, 2, half, width), lambda i: (0, 0, 0, i)),
            pl.BlockSpec(pick.shape, whole),
            pl.BlockSpec(pick.shape[::-1], whole),
        ],
        out_specs=[block, side, side],
        out_shape=[jax.ShapeDtypeStruct(base.shape, jnp.float32), side_shape, side_shape],
        compiler_params=pltpu.CompilerParams(vmem_limit_bytes=VMEM_BYTES),
        cost_estimate=pl.CostEstimate(flops=4 << 20, bytes_accessed=4 << 20, transcendentals=0),
        name="update_border",
    )(base, *sides, primal, jnp.asarray(pick), jnp.asarray(pick.T))


def finish_kernel(
    me_ref, image_a_ref, base_b_ref, own_ref, one_ref, two_ref, three_ref, primal_ref,
    dual_ref, rows_ref, columns_ref, image_ref, update_ref, mid_ref, back_ref,
):
    step = pl.program_id(0)
    channels, _, half, width = image_ref.shape
    edge = LANES
    columns = mid_ref.shape[2] - 2 * edge
    blocks = columns // width

    @pl.when(step == 0)
    def _():
        zeros = jnp.zeros(mid_ref.shape[:2] + (edge,), mid_ref.dtype)
        mid_ref[:, :, :edge] = zeros
        mid_ref[:, :, edge + columns :] = zeros

    for part, part_ref in enumerate((own_ref, one_ref, two_ref, three_ref)):

        @pl.when((step ^ me_ref[0]) == part)
        def _(part_ref=part_ref):
            back_ref[...] = part_ref[...].reshape(back_ref.shape)

    @pl.when(step < blocks)
    def _():
        image_b = jnp.maximum(base_b_ref[...] - STEP_PRIMAL * back_ref[...], 0.0)
        image_a = image_a_ref[...]
        wide_a = image_a.reshape(channels, half, width)
        wide_b = image_b.reshape(channels, half, width)
        first = lax.broadcasted_iota(jnp.int32, wide_a.shape, 1) < half // 2
        image_ref[:, 0] = jnp.where(first, wide_a, wide_b)
        image_ref[:, 1] = jnp.where(first, wide_b, wide_a)
        primal = primal_ref[...]
        stacked = jnp.concatenate(
            [
                2.0 * image_a - pick_part(primal, 0),
                2.0 * image_b - pick_part(primal, 1),
            ],
            axis=0,
        )
        high, low = split(product_left(rows_ref, stacked))
        at = pl.ds(pl.multiple_of(edge + step * width, LANES), width)
        mid_ref[0, :, at] = high
        mid_ref[1, :, at] = low

    rows = mid_ref.shape[1] // 2

    @pl.when(step > 0)
    def _():
        for block in range(width // (2 * LANES)):
            start = pl.multiple_of((step - 1) * width + block * 2 * LANES, LANES)
            high = mid_ref[0, :, pl.ds(start, 4 * LANES)]
            low = mid_ref[1, :, pl.ds(start, 4 * LANES)]
            both = product(high, columns_ref[0]) + product(low, columns_ref[0])
            both = both + product(high, columns_ref[1])
            out = slice(block * LANES, (block + 1) * LANES)
            for band in range(4):
                here = slice(band // 2 * rows, (band // 2 + 1) * rows)
                cols = slice(band % 2 * LANES, (band % 2 + 1) * LANES)
                update_ref[band, :, out] = dual_ref[band, :, out] + STEP_DUAL * both[here, cols]


def finish(me, image_a, base_b, parts, core_b, far_b, primal, dual):
    channels, _, half, columns = primal.shape
    rows = split_constant(analysis_rows(channels, 2 * half)[:, : 2 * channels * half])
    taps_across = split_constant(analysis_columns())
    blocks = parts.shape[0]
    width = columns // blocks
    pixels = channels * half
    now = lambda i, me: (0, jnp.minimum(i, blocks - 1))
    now4 = lambda i, me: (0, 0, 0, jnp.minimum(i, blocks - 1))
    before = lambda i, me: (0, 0, jnp.maximum(i - 1, 0))
    whole3 = lambda i, me: (0, 0, 0)
    part = pl.BlockSpec((pixels, width), now)
    return pl.pallas_call(
        finish_kernel,
        grid_spec=pltpu.PrefetchScalarGridSpec(
            num_scalar_prefetch=1,
            grid=(blocks + 1,),
            in_specs=[
                part,
                part,
                own_part(parts, 1),
                pl.BlockSpec((1, pixels, width), whole3),
                pl.BlockSpec((1, pixels, width), whole3),
                pl.BlockSpec((1, pixels, width), lambda i, me: (1, 0, 0)),
                pl.BlockSpec((channels, 2, half, width), now4),
                pl.BlockSpec((4, pixels, width // 2), before),
                pl.BlockSpec(rows.shape, whole3),
                pl.BlockSpec(taps_across.shape, whole3),
            ],
            out_specs=[
                pl.BlockSpec((channels, 2, half, width), now4),
                pl.BlockSpec((4, pixels, width // 2), before),
            ],
            scratch_shapes=[
                pltpu.VMEM((2, rows.shape[1], columns + 2 * LANES), jnp.bfloat16),
                pltpu.VMEM((pixels, width), jnp.float32),
            ],
        ),
        out_shape=[
            jax.ShapeDtypeStruct(primal.shape, jnp.float32),
            jax.ShapeDtypeStruct(dual.shape, jnp.float32),
        ],
        compiler_params=pltpu.CompilerParams(vmem_limit_bytes=VMEM_BYTES),
        cost_estimate=pl.CostEstimate(flops=4 << 30, bytes_accessed=12 << 20, transcendentals=0),
        name="finish",
    )(me, image_a, base_b, parts, core_b, far_b, far_b, primal, dual, rows, taps_across)


def halo_kernel(
    main_ref, above_ref, below_ref, rows_ref, columns_ref, update_ref, squares_ref, mid_ref
):
    step = pl.program_id(0)
    edge = LANES
    columns = above_ref.shape[1]
    _, _, width = update_ref.shape
    half = squares_ref.shape[1]
    count = mid_ref.shape[0] // 2

    @pl.when(step == 0)
    def _():
        zeros = jnp.zeros((2 * count, edge), mid_ref.dtype)
        mid_ref[:, :edge] = zeros
        mid_ref[:, edge + columns :] = zeros
        high, low = split(jnp.concatenate([above_ref[...], below_ref[...]], axis=0))
        mid_ref[:count, edge : edge + columns] = high
        mid_ref[count:, edge : edge + columns] = low

    rows = rows_ref.shape[1] // 2
    for block in range(width // LANES):
        start = pl.multiple_of(2 * (step * width + block * LANES), LANES)
        window = mid_ref[:, pl.ds(start, 4 * LANES)]
        once = product(window, columns_ref[0])
        across = once[:count] + once[count:] + product(window[:count], columns_ref[1])
        both = product_left(rows_ref, across)
        out = slice(block * LANES, (block + 1) * LANES)
        for band in range(4):
            here = slice(band // 2 * rows, (band // 2 + 1) * rows)
            cols = slice(band % 2 * LANES, (band % 2 + 1) * LANES)
            update = main_ref[band, :, out] + STEP_DUAL * both[here, cols]
            update_ref[band, :, out] = update
            squares = update * update
            squares_ref[band, :, out] = jnp.sum(squares.reshape(-1, half, LANES), axis=0)


def add_halo(main, above, below, half):
    _, pixels, columns = main.shape
    channels = pixels // half
    rows = split_constant(analysis_rows(channels, 2 * half)[:, 2 * pixels :])
    taps_across = split_constant(analysis_columns())
    blocks = 2
    wide = pl.BlockSpec((4, pixels, columns // blocks), lambda i: (0, 0, i))
    whole = lambda i: (0, 0)
    whole3 = lambda i: (0, 0, 0)
    return pl.pallas_call(
        halo_kernel,
        grid=(blocks,),
        in_specs=[
            wide,
            pl.BlockSpec(above.shape, whole),
            pl.BlockSpec(below.shape, whole),
            pl.BlockSpec(rows.shape, whole3),
            pl.BlockSpec(taps_across.shape, whole3),
        ],
        out_specs=[wide, pl.BlockSpec((4, half, columns // blocks), lambda i: (0, 0, i))],
        out_shape=[
            jax.ShapeDtypeStruct(main.shape, jnp.float32),
            jax.ShapeDtypeStruct((4, half, columns), jnp.float32),
        ],
        scratch_shapes=[pltpu.VMEM((4 * above.shape[0], above.shape[1] + 2 * LANES), jnp.bfloat16)],
        compiler_params=pltpu.CompilerParams(vmem_limit_bytes=VMEM_BYTES),
        cost_estimate=pl.CostEstimate(flops=1 << 30, bytes_accessed=5 << 20, transcendentals=0),
        name="add_halo",
    )(main, above, below, rows, taps_across)


def project_kernel(update_ref, weight_ref, sums_ref, out_ref):
    total = (sums_ref[0, 0] + sums_ref[1, 0]) + (sums_ref[2, 0] + sums_ref[3, 0])
    weight = weight_ref[0]
    factor = weight / jnp.maximum(jnp.sqrt(total), weight)
    count = factor.shape[0]
    for channel in range(update_ref.shape[1] // count):
        rows = slice(channel * count, (channel + 1) * count)
        out_ref[0, rows, :] = update_ref[0, rows, :] * factor


def project(update, weight, sums):
    bands, pixels, columns = update.shape
    half = weight.shape[1]
    wide = pl.BlockSpec((1, pixels, columns), lambda i: (i, 0, 0))
    return pl.pallas_call(
        project_kernel,
        grid=(bands,),
        in_specs=[
            wide,
            pl.BlockSpec((1, half, columns), lambda i: (i, 0, 0)),
            pl.BlockSpec((sums.shape[0], 1, half, columns), lambda i: (0, i, 0, 0)),
        ],
        out_specs=wide,
        out_shape=jax.ShapeDtypeStruct(update.shape, jnp.float32),
        compiler_params=pltpu.CompilerParams(vmem_limit_bytes=VMEM_BYTES),
        cost_estimate=pl.CostEstimate(flops=4 << 20, bytes_accessed=5 << 20, transcendentals=0),
        name="project",
    )(update, weight, sums)


def shards(
    primal_image, dual_coef, l21_weight, visibilities, tile_index, kernel_values, kernel_pattern
):
    facets, groups = lax.axis_size("fac"), lax.axis_size("chan")
    channels, rows, columns = primal_image.shape
    quarter = columns // groups
    half = rows // 2
    forward = [(i, i + 1) for i in range(facets - 1)]
    backward = [(b, a) for a, b in forward]
    me = lax.axis_index("chan")
    primal = primal_image.reshape(channels, 2, half, columns)
    dual = dual_coef.reshape(4, channels * half, columns // 2)

    grid = back_project(
        visibilities, tile_index, kernel_values[0], kernel_pattern[0], rows, facets, quarter
    )
    by_facet = lax.all_to_all(
        grid.reshape(facets, rows, quarter), "fac", split_axis=0, concat_axis=0, tiled=True
    )
    dual_here, _ = lax.optimization_barrier((dual, grid))
    base_a, base_b, to_above, to_below = synthesize(dual_here, primal)
    near = [pair for pair in forward if pair[1] % RING != 0]
    far = [pair for pair in forward if pair[1] % RING == 0]
    turned = lambda those: [(b, a) for a, b in those]
    far_sides = [lax.ppermute(to_below, "fac", far), lax.ppermute(to_above, "fac", turned(far))]
    by_facet, to_above, to_below = lax.optimization_barrier((by_facet, to_above, to_below))
    sides = [lax.ppermute(to_below, "fac", near), lax.ppermute(to_above, "fac", turned(near))]
    parts = by_facet.reshape(groups, channels, 2, half, quarter)

    def piece(part, step):
        return lax.dynamic_index_in_dim(parts[:, :, part], me ^ step, 0, False).reshape(-1, quarter)

    def pairs(step):
        return [(i, i ^ step) for i in range(groups)]

    sent_a = [piece(0, step) for step in (1, 2, 3)]
    sent_b = jnp.stack([piece(1, 1), piece(1, 3)])
    kept_b = piece(1, 2)
    sent_a, sent_b, kept_b = lax.optimization_barrier((sent_a, sent_b, kept_b))
    backs_a = [lax.ppermute(sent_a[step - 1], "chan", pairs(step)) for step in (1, 2, 3)]
    core_b = lax.ppermute(sent_b, "chan", pairs(1))
    far_b = lax.ppermute(jnp.stack([kept_b, core_b[1]]), "chan", pairs(2))
    me = me.astype(jnp.int32).reshape(1)
    image_a, first, last = update_border(
        border_sum(me, add_sides(base_a, *far_sides), parts, backs_a), sides, primal
    )
    above = lax.ppermute(last, "fac", forward)
    below = lax.ppermute(first, "fac", backward)
    image, main = finish(me, image_a, base_b, parts, core_b, far_b, primal, dual)
    update, squares = add_halo(main, above, below, half)
    sums = lax.all_gather(squares, "chan")
    dual_next = project(update, l21_weight, sums)
    return (image.reshape(primal_image.shape), dual_next.reshape(dual_coef.shape))


def solution(mesh):
    in_specs = (
        P("chan", "fac", None),
        P(None, "chan", "fac", None),
        P(None, "fac", None),
        P("fac", "chan"),
        P("fac", "chan"),
        P("fac", "chan", None),
        P("fac", "chan", None),
    )
    out_specs = (P("chan", "fac", None), P(None, "chan", "fac", None))
    return jax.shard_map(shards, mesh=mesh, in_specs=in_specs, out_specs=out_specs, check_vma=False)
```

```python
import functools

import jax
import jax.numpy as jnp
import ml_dtypes
import numpy as np
from jax import lax
from jax.experimental import pallas as pl
from jax.experimental.pallas import tpu as pltpu
from jax.sharding import PartitionSpec as P

FILTER_LOW = [
    0.23037781330885523,
    0.7148465705525415,
    0.6308807679295904,
    -0.02798376941698385,
    -0.18703481171888114,
    0.030841381835986965,
    0.032883011666982945,
    -0.010597401784997278,
]
FILTER_HIGH = [(-1.0) ** offset * FILTER_LOW[7 - offset] for offset in range(8)]
STEP_PRIMAL = 0.5
STEP_DUAL = 1.0
LANES = 128
VMEM_BYTES = 24 * 1024 * 1024
BACK_VMEM_BYTES = 60 * 1024 * 1024
PARTS = 4
RING = 8


def taps(filters, offset):
    table = np.asarray(filters, np.float64)
    valid = (offset >= 0) & (offset < 8)
    return np.where(valid, table[np.clip(offset, 0, 7)], 0.0)


def split_constant(matrix):
    matrix = matrix.astype(np.float32)
    high = matrix.astype(ml_dtypes.bfloat16)
    low = (matrix - high.astype(np.float32)).astype(ml_dtypes.bfloat16)
    return jnp.asarray(np.stack([high, low]))


def split(values):
    high = values.astype(jnp.bfloat16)
    low = (values - high.astype(jnp.float32)).astype(jnp.bfloat16)
    return high, low


def product(a, b):
    return jnp.dot(a, b, preferred_element_type=jnp.float32)


def product_left(matrix, values):
    high, low = split(values)
    return product(matrix[0], high) + product(matrix[0], low) + product(matrix[1], high)


def part_rows(rows):
    half = rows // 2
    a = [row if row < half // 2 else row + half for row in range(half)]
    b = [row + half if row < half // 2 else row for row in range(half)]
    return np.array(a), np.array(b)


def synthesis_rows(channels, rows):
    coef = np.arange(rows // 2)[None, :]
    a, b = part_rows(rows)
    sides = (-3, -2, -1, rows, rows + 1, rows + 2)
    blocks = []
    for filters in (FILTER_LOW, FILTER_HIGH):
        parts = [np.kron(np.eye(channels), taps(filters, p[:, None] - 2 * coef + 3)) for p in (a, b)]
        parts += [np.kron(np.eye(channels), taps(filters, row - 2 * coef + 3)) for row in sides]
        blocks.append(np.concatenate(parts, axis=0))
    return np.concatenate(blocks, axis=1)


def synthesis_columns():
    coef = np.arange(3 * LANES)[:, None] - LANES
    pixel = np.arange(2 * LANES)[None, :]
    return np.concatenate(
        [taps(filters, pixel - 2 * coef + 3) for filters in (FILTER_LOW, FILTER_HIGH)], axis=0
    )


def analysis_rows(channels, rows):
    coef = np.arange(rows // 2)[:, None]
    a, b = part_rows(rows)
    sides = (-3, -2, -1, rows, rows + 1, rows + 2)
    bands = []
    for filters in (FILTER_LOW, FILTER_HIGH):
        parts = [np.kron(np.eye(channels), taps(filters, p[None, :] - 2 * coef + 3)) for p in (a, b)]
        parts += [np.kron(np.eye(channels), taps(filters, row - 2 * coef + 3)) for row in sides]
        bands.append(np.concatenate(parts, axis=1))
    return np.concatenate(bands, axis=0)


def analysis_columns():
    pixel = np.arange(4 * LANES)[:, None] - LANES
    coef = np.arange(LANES)[None, :]
    return np.concatenate(
        [taps(filters, pixel - 2 * coef + 3) for filters in (FILTER_LOW, FILTER_HIGH)], axis=1
    )


def border_rows(channels, rows):
    a, _ = part_rows(rows)
    ends = (0, 1, 2, rows - 3, rows - 2, rows - 1)
    picked = [np.kron(np.eye(channels), a[None, :] == row) for row in ends]
    return np.concatenate(picked, axis=0).astype(ml_dtypes.bfloat16)


def back_kernel(
    vis_ref, tile_ref, kernel_hbm, pattern_hbm, out_hbm,
    kernel_ref, pattern_ref, cells_ref, out_ref, sems, out_sems, *, rows,
):
    count = tile_ref.shape[1]
    step = 1024
    steps = count // step
    half = rows // 2
    parts = out_ref.shape[0]
    slots = out_ref.shape[1]

    def copies(index):
        at = pl.ds(index * step, step)
        return (
            pltpu.make_async_copy(pattern_hbm.at[at, :], pattern_ref.at[at, :], sems.at[0, index]),
            pltpu.make_async_copy(kernel_hbm.at[at, :], kernel_ref.at[at, :], sems.at[1, index]),
        )

    def copy_out(part):
        return pltpu.make_async_copy(
            out_ref.at[part], out_hbm.at[pl.ds(part * slots, slots), :], out_sems.at[part]
        )

    for index in range(steps):
        for copy in copies(index):
            copy.start()

    tile = tile_ref[...]
    row = tile >> 2
    within = row & (rows - 1)
    in_b = ((within >> 2) ^ (within >> 3)) & 1
    place = (row - within) + half * in_b + (within & (half - 1))
    iota = lax.broadcasted_iota(jnp.int32, (slots, step), 0).astype(jnp.float32).astype(jnp.bfloat16)
    values = vis_ref[...]
    zero = jnp.zeros((), jnp.bfloat16)

    for part in range(parts):
        total = None
        for index in range(steps):
            at = slice(index * step, (index + 1) * step)
            if part == 0:
                for copy in copies(index):
                    copy.wait()
                lane_tile = jnp.transpose(jnp.broadcast_to(tile[:, at] & 3, (LANES, step)))
                kept = jnp.where(pattern_ref[at, :] != 0, lane_tile, 4)
                kept = kept.astype(jnp.float32).astype(jnp.bfloat16)
                kernels = kernel_ref[at, :]
                for column in range(4):
                    cells_ref[at, column * LANES : (column + 1) * LANES] = jnp.where(
                        kept == column, kernels, zero
                    )
            local = place[:, at] - part * slots
            local = jnp.where((local >= 0) & (local < slots), local, -1)
            local = local.astype(jnp.float32).astype(jnp.bfloat16)
            spread = jnp.where(local == iota, values[:, at], zero)
            term = product(spread, cells_ref[at, :])
            total = term if total is None else total + term
        out_ref[part] = total
        copy_out(part).start()
    for part in range(parts):
        copy_out(part).wait()


def back_project(vis, tile, kernels, pattern, rows, facets, quarter):
    count = tile.shape[1]
    parts = PARTS
    slots = rows * facets // parts
    vmem = pl.BlockSpec(memory_space=pltpu.VMEM)
    hbm = pl.BlockSpec(memory_space=pl.ANY)
    return pl.pallas_call(
        functools.partial(back_kernel, rows=rows),
        in_specs=[vmem, vmem, hbm, hbm],
        out_specs=hbm,
        out_shape=jax.ShapeDtypeStruct((rows * facets, quarter), jnp.float32),
        scratch_shapes=[
            pltpu.VMEM((count, LANES), kernels.dtype),
            pltpu.VMEM((count, LANES), pattern.dtype),
            pltpu.VMEM((count, quarter), jnp.bfloat16),
            pltpu.VMEM((parts, slots, quarter), jnp.float32),
            pltpu.SemaphoreType.DMA((2, count // 1024)),
            pltpu.SemaphoreType.DMA((parts,)),
        ],
        compiler_params=pltpu.CompilerParams(vmem_limit_bytes=BACK_VMEM_BYTES),
        cost_estimate=pl.CostEstimate(
            flops=2 * rows * facets * count * quarter, bytes_accessed=6 << 20, transcendentals=0
        ),
        name="back_project",
    )(vis, tile, kernels, pattern)


def pick_part(natural, part):
    half = natural.shape[2]
    first = lax.broadcasted_iota(jnp.int32, natural[:, 0].shape, 1) < half // 2
    one, two = (natural[:, 0], natural[:, 1]) if part == 0 else (natural[:, 1], natural[:, 0])
    return jnp.where(first, one, two).reshape(-1, natural.shape[3])


def synthesis_kernel(dual_ref, primal_ref, rows_ref, columns_ref, a_ref, b_ref, above_ref, below_ref, mid_ref):
    tiles = dual_ref.shape[2] // LANES
    for kind in range(2):
        for at in range(0, tiles, 2):
            lanes = slice(at * LANES, (at + 2) * LANES)
            stacked = jnp.concatenate([dual_ref[kind, :, lanes], dual_ref[kind + 2, :, lanes]], axis=0)
            high, low = split(product_left(rows_ref, stacked))
            mid_ref[kind, 0, :, lanes] = high
            mid_ref[kind, 1, :, lanes] = low
    half = a_ref.shape[0]
    side = above_ref.shape[0]
    for at in range(tiles):
        first, last = max(at - 1, 0), min(at + 2, tiles)
        lanes = slice(first * LANES, last * LANES)
        total = 0.0
        for kind in range(2):
            base = (3 * kind + first - at + 1) * LANES
            part = slice(base, base + (last - first) * LANES)
            total = total + product(mid_ref[kind, 0, :, lanes], columns_ref[0, part, :])
            total = total + product(mid_ref[kind, 1, :, lanes], columns_ref[0, part, :])
            total = total + product(mid_ref[kind, 0, :, lanes], columns_ref[1, part, :])
        pixels = slice(2 * at * LANES, 2 * (at + 1) * LANES)
        primal = primal_ref[:, :, :, pixels]
        a_ref[:, pixels] = pick_part(primal, 0) - STEP_PRIMAL * total[:half]
        b_ref[:, pixels] = pick_part(primal, 1) - STEP_PRIMAL * total[half : 2 * half]
        above_ref[:, pixels] = total[2 * half : 2 * half + side]
        below_ref[:, pixels] = total[2 * half + side :]


def synthesize(dual, primal):
    channels, _, half, columns = primal.shape
    part = jax.ShapeDtypeStruct((channels * half, columns), jnp.float32)
    side = jax.ShapeDtypeStruct((3 * channels, columns), jnp.float32)
    rows = split_constant(synthesis_rows(channels, 2 * half))
    return pl.pallas_call(
        synthesis_kernel,
        out_shape=[part, part, side, side],
        scratch_shapes=[pltpu.VMEM((2, 2, rows.shape[1], columns // 2), jnp.bfloat16)],
        compiler_params=pltpu.CompilerParams(vmem_limit_bytes=VMEM_BYTES),
        cost_estimate=pl.CostEstimate(flops=8 << 30, bytes_accessed=8 << 20, transcendentals=0),
        name="synthesis",
    )(dual, primal, rows, split_constant(synthesis_columns()))


def own_part(parts, part):
    _, channels, _, half, quarter = parts.shape
    return pl.BlockSpec((1, channels, 1, half, quarter), lambda i, me: (me[0], 0, part, 0, 0))


def sides_kernel(base_ref, above_ref, below_ref, place_ref, out_ref):
    high, low = split(jnp.concatenate([above_ref[...], below_ref[...]], axis=0))
    added = product(place_ref[...], high) + product(place_ref[...], low)
    out_ref[...] = base_ref[...] - STEP_PRIMAL * added


def add_sides(base, above, below):
    pixels, columns = base.shape
    channels = above.shape[0] // 3
    place = border_rows(channels, 2 * pixels // channels).T
    return pl.pallas_call(
        sides_kernel,
        out_shape=jax.ShapeDtypeStruct(base.shape, jnp.float32),
        compiler_params=pltpu.CompilerParams(vmem_limit_bytes=VMEM_BYTES),
        cost_estimate=pl.CostEstimate(flops=40 << 30, bytes_accessed=3 << 20, transcendentals=0),
        name="add_sides",
    )(base, above, below, jnp.asarray(place))


def border_sum_kernel(me_ref, base_ref, own_ref, one_ref, two_ref, three_ref, out_ref):
    for step, back_ref in enumerate((own_ref, one_ref, two_ref, three_ref)):

        @pl.when(pl.program_id(0) == step)
        def _(back_ref=back_ref):
            out_ref[...] = base_ref[...] - STEP_PRIMAL * back_ref[...].reshape(base_ref.shape)


def border_sum(me, base, parts, backs):
    pixels, columns = base.shape
    groups = parts.shape[0]
    quarter = columns // groups
    block = pl.BlockSpec((pixels, quarter), lambda i, me: (0, i ^ me[0]))
    whole = lambda i, me: (0, 0)
    return pl.pallas_call(
        border_sum_kernel,
        grid_spec=pltpu.PrefetchScalarGridSpec(
            num_scalar_prefetch=1,
            grid=(groups,),
            in_specs=[block, own_part(parts, 0)]
            + [pl.BlockSpec((pixels, quarter), whole)] * len(backs),
            out_specs=block,
        ),
        out_shape=jax.ShapeDtypeStruct(base.shape, jnp.float32),
        compiler_params=pltpu.CompilerParams(vmem_limit_bytes=VMEM_BYTES),
        cost_estimate=pl.CostEstimate(flops=6 << 30, bytes_accessed=3 << 20, transcendentals=0),
        name="border_sum",
    )(me, base, parts, *backs)


def border_kernel(
    base_ref, above_ref, below_ref, primal_ref, pick_ref, place_ref, image_ref, first_ref, last_ref
):
    high, low = split(jnp.concatenate([above_ref[...], below_ref[...]], axis=0))
    added = product(place_ref[...], high) + product(place_ref[...], low)
    image = jnp.maximum(base_ref[...] - STEP_PRIMAL * added, 0.0)
    image_ref[...] = image
    high, low = split(2.0 * image - pick_part(primal_ref[...], 0))
    picked = product(pick_ref[...], high) + product(pick_ref[...], low)
    half = picked.shape[0] // 2
    first_ref[...] = picked[:half]
    last_ref[...] = picked[half:]


def update_border(base, sides, primal):
    pixels, columns = base.shape
    channels, _, half, _ = primal.shape
    blocks = 2
    width = columns // blocks
    pick = border_rows(channels, 2 * half)
    block = pl.BlockSpec((pixels, width), lambda i: (0, i))
    side = pl.BlockSpec((3 * channels, width), lambda i: (0, i))
    whole = lambda i: (0, 0)
    side_shape = jax.ShapeDtypeStruct((3 * channels, columns), jnp.float32)
    return pl.pallas_call(
        border_kernel,
        grid=(blocks,),
        in_specs=[
            block,
            side,
            side,
            pl.BlockSpec((channels, 2, half, width), lambda i: (0, 0, 0, i)),
            pl.BlockSpec(pick.shape, whole),
            pl.BlockSpec(pick.shape[::-1], whole),
        ],
        out_specs=[block, side, side],
        out_shape=[jax.ShapeDtypeStruct(base.shape, jnp.float32), side_shape, side_shape],
        compiler_params=pltpu.CompilerParams(vmem_limit_bytes=VMEM_BYTES),
        cost_estimate=pl.CostEstimate(flops=4 << 20, bytes_accessed=4 << 20, transcendentals=0),
        name="update_border",
    )(base, *sides, primal, jnp.asarray(pick), jnp.asarray(pick.T))


def finish_kernel(
    me_ref, image_a_ref, base_b_ref, own_ref, one_ref, two_ref, three_ref, primal_ref,
    dual_ref, rows_ref, columns_ref, image_ref, update_ref, mid_ref, back_ref,
):
    step = pl.program_id(0)
    channels, _, half, width = image_ref.shape
    edge = LANES
    columns = mid_ref.shape[2] - 2 * edge
    blocks = columns // width

    @pl.when(step == 0)
    def _():
        zeros = jnp.zeros(mid_ref.shape[:2] + (edge,), mid_ref.dtype)
        mid_ref[:, :, :edge] = zeros
        mid_ref[:, :, edge + columns :] = zeros

    for part, part_ref in enumerate((own_ref, one_ref, two_ref, three_ref)):

        @pl.when((step ^ me_ref[0]) == part)
        def _(part_ref=part_ref):
            back_ref[...] = part_ref[...].reshape(back_ref.shape)

    @pl.when(step < blocks)
    def _():
        image_b = jnp.maximum(base_b_ref[...] - STEP_PRIMAL * back_ref[...], 0.0)
        image_a = image_a_ref[...]
        wide_a = image_a.reshape(channels, half, width)
        wide_b = image_b.reshape(channels, half, width)
        first = lax.broadcasted_iota(jnp.int32, wide_a.shape, 1) < half // 2
        image_ref[:, 0] = jnp.where(first, wide_a, wide_b)
        image_ref[:, 1] = jnp.where(first, wide_b, wide_a)
        primal = primal_ref[...]
        stacked = jnp.concatenate(
            [
                2.0 * image_a - pick_part(primal, 0),
                2.0 * image_b - pick_part(primal, 1),
            ],
            axis=0,
        )
        high, low = split(product_left(rows_ref, stacked))
        at = pl.ds(pl.multiple_of(edge + step * width, LANES), width)
        mid_ref[0, :, at] = high
        mid_ref[1, :, at] = low

    rows = mid_ref.shape[1] // 2

    @pl.when(step > 0)
    def _():
        for block in range(width // (2 * LANES)):
            start = pl.multiple_of((step - 1) * width + block * 2 * LANES, LANES)
            high = mid_ref[0, :, pl.ds(start, 4 * LANES)]
            low = mid_ref[1, :, pl.ds(start, 4 * LANES)]
            both = product(high, columns_ref[0]) + product(low, columns_ref[0])
            both = both + product(high, columns_ref[1])
            out = slice(block * LANES, (block + 1) * LANES)
            for band in range(4):
                here = slice(band // 2 * rows, (band // 2 + 1) * rows)
                cols = slice(band % 2 * LANES, (band % 2 + 1) * LANES)
                update_ref[band, :, out] = dual_ref[band, :, out] + STEP_DUAL * both[here, cols]


def finish(me, image_a, base_b, parts, core_b, far_b, primal, dual):
    channels, _, half, columns = primal.shape
    rows = split_constant(analysis_rows(channels, 2 * half)[:, : 2 * channels * half])
    taps_across = split_constant(analysis_columns())
    blocks = parts.shape[0]
    width = columns // blocks
    pixels = channels * half
    now = lambda i, me: (0, jnp.minimum(i, blocks - 1))
    now4 = lambda i, me: (0, 0, 0, jnp.minimum(i, blocks - 1))
    before = lambda i, me: (0, 0, jnp.maximum(i - 1, 0))
    whole3 = lambda i, me: (0, 0, 0)
    part = pl.BlockSpec((pixels, width), now)
    return pl.pallas_call(
        finish_kernel,
        grid_spec=pltpu.PrefetchScalarGridSpec(
            num_scalar_prefetch=1,
            grid=(blocks + 1,),
            in_specs=[
                part,
                part,
                own_part(parts, 1),
                pl.BlockSpec((1, pixels, width), whole3),
                pl.BlockSpec((1, pixels, width), whole3),
                pl.BlockSpec((1, pixels, width), lambda i, me: (1, 0, 0)),
                pl.BlockSpec((channels, 2, half, width), now4),
                pl.BlockSpec((4, pixels, width // 2), before),
                pl.BlockSpec(rows.shape, whole3),
                pl.BlockSpec(taps_across.shape, whole3),
            ],
            out_specs=[
                pl.BlockSpec((channels, 2, half, width), now4),
                pl.BlockSpec((4, pixels, width // 2), before),
            ],
            scratch_shapes=[
                pltpu.VMEM((2, rows.shape[1], columns + 2 * LANES), jnp.bfloat16),
                pltpu.VMEM((pixels, width), jnp.float32),
            ],
        ),
        out_shape=[
            jax.ShapeDtypeStruct(primal.shape, jnp.float32),
            jax.ShapeDtypeStruct(dual.shape, jnp.float32),
        ],
        compiler_params=pltpu.CompilerParams(vmem_limit_bytes=VMEM_BYTES),
        cost_estimate=pl.CostEstimate(flops=4 << 30, bytes_accessed=12 << 20, transcendentals=0),
        name="finish",
    )(me, image_a, base_b, parts, core_b, far_b, far_b, primal, dual, rows, taps_across)


def halo_kernel(
    main_ref, above_ref, below_ref, rows_ref, columns_ref, update_ref, squares_ref, mid_ref
):
    step = pl.program_id(0)
    edge = LANES
    columns = above_ref.shape[1]
    _, _, width = update_ref.shape
    half = squares_ref.shape[1]
    count = mid_ref.shape[0] // 2

    @pl.when(step == 0)
    def _():
        zeros = jnp.zeros((2 * count, edge), mid_ref.dtype)
        mid_ref[:, :edge] = zeros
        mid_ref[:, edge + columns :] = zeros
        high, low = split(jnp.concatenate([above_ref[...], below_ref[...]], axis=0))
        mid_ref[:count, edge : edge + columns] = high
        mid_ref[count:, edge : edge + columns] = low

    rows = rows_ref.shape[1] // 2
    for block in range(width // LANES):
        start = pl.multiple_of(2 * (step * width + block * LANES), LANES)
        window = mid_ref[:, pl.ds(start, 4 * LANES)]
        once = product(window, columns_ref[0])
        across = once[:count] + once[count:] + product(window[:count], columns_ref[1])
        both = product_left(rows_ref, across)
        out = slice(block * LANES, (block + 1) * LANES)
        for band in range(4):
            here = slice(band // 2 * rows, (band // 2 + 1) * rows)
            cols = slice(band % 2 * LANES, (band % 2 + 1) * LANES)
            update = main_ref[band, :, out] + STEP_DUAL * both[here, cols]
            update_ref[band, :, out] = update
            squares = update * update
            squares_ref[band, :, out] = jnp.sum(squares.reshape(-1, half, LANES), axis=0)


def add_halo(main, above, below, half):
    _, pixels, columns = main.shape
    channels = pixels // half
    rows = split_constant(analysis_rows(channels, 2 * half)[:, 2 * pixels :])
    taps_across = split_constant(analysis_columns())
    blocks = 2
    wide = pl.BlockSpec((4, pixels, columns // blocks), lambda i: (0, 0, i))
    whole = lambda i: (0, 0)
    whole3 = lambda i: (0, 0, 0)
    return pl.pallas_call(
        halo_kernel,
        grid=(blocks,),
        in_specs=[
            wide,
            pl.BlockSpec(above.shape, whole),
            pl.BlockSpec(below.shape, whole),
            pl.BlockSpec(rows.shape, whole3),
            pl.BlockSpec(taps_across.shape, whole3),
        ],
        out_specs=[wide, pl.BlockSpec((4, half, columns // blocks), lambda i: (0, 0, i))],
        out_shape=[
            jax.ShapeDtypeStruct(main.shape, jnp.float32),
            jax.ShapeDtypeStruct((4, half, columns), jnp.float32),
        ],
        scratch_shapes=[pltpu.VMEM((4 * above.shape[0], above.shape[1] + 2 * LANES), jnp.bfloat16)],
        compiler_params=pltpu.CompilerParams(vmem_limit_bytes=VMEM_BYTES),
        cost_estimate=pl.CostEstimate(flops=1 << 30, bytes_accessed=5 << 20, transcendentals=0),
        name="add_halo",
    )(main, above, below, rows, taps_across)


def project_kernel(update_ref, weight_ref, sums_ref, out_ref):
    total = (sums_ref[0] + sums_ref[1]) + (sums_ref[2] + sums_ref[3])
    weight = weight_ref[...]
    factor = weight / jnp.maximum(jnp.sqrt(total), weight)
    count = factor.shape[1]
    for channel in range(update_ref.shape[1] // count):
        rows = slice(channel * count, (channel + 1) * count)
        out_ref[:, rows, :] = update_ref[:, rows, :] * factor


def project(update, weight, sums):
    bands, pixels, columns = update.shape
    half = weight.shape[1]
    each = 2
    wide = pl.BlockSpec((each, pixels, columns), lambda i: (i, 0, 0))
    return pl.pallas_call(
        project_kernel,
        grid=(bands // each,),
        in_specs=[
            wide,
            pl.BlockSpec((each, half, columns), lambda i: (i, 0, 0)),
            pl.BlockSpec((sums.shape[0], each, half, columns), lambda i: (0, i, 0, 0)),
        ],
        out_specs=wide,
        out_shape=jax.ShapeDtypeStruct(update.shape, jnp.float32),
        compiler_params=pltpu.CompilerParams(vmem_limit_bytes=VMEM_BYTES),
        cost_estimate=pl.CostEstimate(flops=4 << 20, bytes_accessed=5 << 20, transcendentals=0),
        name="project",
    )(update, weight, sums)


def shards(
    primal_image, dual_coef, l21_weight, visibilities, tile_index, kernel_values, kernel_pattern
):
    facets, groups = lax.axis_size("fac"), lax.axis_size("chan")
    channels, rows, columns = primal_image.shape
    quarter = columns // groups
    half = rows // 2
    forward = [(i, i + 1) for i in range(facets - 1)]
    backward = [(b, a) for a, b in forward]
    me = lax.axis_index("chan")
    primal = primal_image.reshape(channels, 2, half, columns)
    dual = dual_coef.reshape(4, channels * half, columns // 2)

    grid = back_project(
        visibilities, tile_index, kernel_values[0], kernel_pattern[0], rows, facets, quarter
    )
    by_facet = lax.all_to_all(
        grid.reshape(facets, rows, quarter), "fac", split_axis=0, concat_axis=0, tiled=True
    )
    dual_here, _ = lax.optimization_barrier((dual, grid))
    base_a, base_b, to_above, to_below = synthesize(dual_here, primal)
    near = [pair for pair in forward if pair[1] % RING != 0]
    far = [pair for pair in forward if pair[1] % RING == 0]
    turned = lambda those: [(b, a) for a, b in those]
    far_sides = [lax.ppermute(to_below, "fac", far), lax.ppermute(to_above, "fac", turned(far))]
    by_facet, to_above, to_below = lax.optimization_barrier((by_facet, to_above, to_below))
    sides = [lax.ppermute(to_below, "fac", near), lax.ppermute(to_above, "fac", turned(near))]
    parts = by_facet.reshape(groups, channels, 2, half, quarter)

    def piece(part, step):
        return lax.dynamic_index_in_dim(parts[:, :, part], me ^ step, 0, False).reshape(-1, quarter)

    def pairs(step):
        return [(i, i ^ step) for i in range(groups)]

    sent_a = [piece(0, step) for step in (1, 2, 3)]
    sent_b = jnp.stack([piece(1, 1), piece(1, 3)])
    kept_b = piece(1, 2)
    sent_a, sent_b, kept_b = lax.optimization_barrier((sent_a, sent_b, kept_b))
    backs_a = [lax.ppermute(sent_a[step - 1], "chan", pairs(step)) for step in (1, 2, 3)]
    core_b = lax.ppermute(sent_b, "chan", pairs(1))
    far_b = lax.ppermute(jnp.stack([kept_b, core_b[1]]), "chan", pairs(2))
    me = me.astype(jnp.int32).reshape(1)
    image_a, first, last = update_border(
        border_sum(me, add_sides(base_a, *far_sides), parts, backs_a), sides, primal
    )
    above = lax.ppermute(last, "fac", forward)
    below = lax.ppermute(first, "fac", backward)
    image, main = finish(me, image_a, base_b, parts, core_b, far_b, primal, dual)
    update, squares = add_halo(main, above, below, half)
    sums = lax.all_gather(squares, "chan")
    dual_next = project(update, l21_weight, sums)
    return (image.reshape(primal_image.shape), dual_next.reshape(dual_coef.shape))


def solution(mesh):
    in_specs = (
        P("chan", "fac", None),
        P(None, "chan", "fac", None),
        P(None, "fac", None),
        P("fac", "chan"),
        P("fac", "chan"),
        P("fac", "chan", None),
        P("fac", "chan", None),
    )
    out_specs = (P("chan", "fac", None), P(None, "chan", "fac", None))
    return jax.shard_map(shards, mesh=mesh, in_specs=in_specs, out_specs=out_specs, check_vma=False)
```
